128 devices in a mesh: dp: 2 (over y_hi), seq: 16 (over x, y_lo, core), tp: 4 (over z).
Axes of the slice: x: 4, y: 4 (y_hi: 2, y_lo: 2; y = y_hi * 2 + y_lo), z: 4, core: 2. Of those that a mesh axis runs over, the one named last changes fastest.
Arguments:
- enc_context: bfloat16 [8, 512, 4096], P('dp', 'seq', 'tp'), may hold values from -6 to 6
- enc_residual: bfloat16 [8, 512, 4096], P('dp', 'seq', 'tp'), may hold values from -96 to 96
- out_weight: bfloat16 [4096, 4096], P('tp'), may hold values from -0.09375 to 0.09375
- norm_gain: float32 [4096], replicated, may hold values from 0.1 to 1.9
- kv_weight: bfloat16 [4096, 2, 4096], P(None, None, 'seq'), may hold values from -0.09375 to 0.09375
- caption_lengths: int32 [8], P(('dp', 'tp')), may hold values from 64 to 512, as said below
- streams: bfloat16 [4, 8, 2048, 4096], P(None, ('dp', 'tp'), 'seq'), may hold values from -96 to 96
- cotangents: bfloat16 [2, 8, 2048, 4096], P(None, ('dp', 'tp'), 'seq'), may hold values from -6 to 6
Outputs:
- self_ctx: bfloat16 [8, 2048, 4096], P(('dp', 'tp'), 'seq')
- cross_ctx: bfloat16 [8, 2048, 4096], P(('dp', 'tp'), 'seq')
- stream_grads: bfloat16 [4, 8, 2048, 4096], P(None, ('dp', 'tp'), 'seq')
- kv_weight_grad: float32 [4096, 2, 4096], P(('dp', 'tp'), None, 'seq')
The draws below stay inside these ranges and needn't reach their ends.
Inputs may be any that keep to these rules, and one draw needn't show every extreme that they name: The first caption_lengths[c] caption tokens of clip c are valid; some caption uses all 512.
All inputs are finite; a program needn't handle non-finite values.
Results may differ from the reference program's by a relative error of at most 0.03035.
Values may be sent and summed in bfloat16 or wider, within the bound.
No kernel may reach another device: no remote copies, remote signals or barrier semaphores. Data moves between devices by JAX's collectives and lax.ppermute only.
A program may use at most 192 MiB of HBM per device.

```python
import math
import jax
import jax.numpy as jnp
from jax import lax

D_TEXT = 4096
HEADS = 32
HD = 128
CAP = 512
CLIPS = 8
CLIP_TOK = 2048


def draw_streams(key, part):
    key = jax.random.fold_in(key, 11)
    shape = (4, CLIPS, CLIP_TOK, HEADS * HD)
    key_base = jax.random.fold_in(key, 0)
    base = jnp.clip(jax.random.normal(key_base, shape, jnp.float32), -5.0, 5.0)
    return base.astype(jnp.bfloat16)


def draw_enc_residual(key, part):
    key = jax.random.fold_in(key, 23)
    key_base, key_rows, key_cols = jax.random.split(key, 3)
    shape = (CLIPS, CAP, D_TEXT)
    ramp = 1.0 + 2.0 * jnp.arange(D_TEXT, dtype=jnp.float32) / (D_TEXT - 1)
    columns = jnp.exp(jax.random.uniform(key_cols, (D_TEXT,), jnp.float32, 0.0, math.log(2.0))) * ramp
    rows = jnp.exp(jax.random.uniform(key_rows, (CLIPS, CAP, 1), jnp.float32, 0.0, math.log(10.0)))
    base = jnp.clip(jax.random.normal(key_base, shape, jnp.float32), -5.0, 5.0)
    return jnp.clip(0.3 * base * rows * columns, -96.0, 96.0).astype(jnp.bfloat16)


def draw_caption_lengths(key, part):
    key = jax.random.fold_in(key, 37)
    key_len, key_order = jax.random.split(key)
    lengths = jax.random.randint(key_len, (CLIPS,), CAP // 8, CAP + 1)
    order = jax.random.permutation(key_order, CLIPS)
    lengths = lengths.at[order[0]].set(CAP).at[order[1]].set(CAP // 8)
    return lengths.astype(jnp.int32)


def block_levels(rng, dims, cuts, low, largest):
    gain = 1.0
    for dim, blocks in cuts:
        heights = jax.random.uniform(jax.random.fold_in(jax.random.fold_in(rng, 6), dim), (blocks,), jnp.float32, low / len(cuts), largest / len(cuts))
        gain = gain * jnp.repeat(jnp.exp(heights), dims[dim] // blocks).reshape((-1,) + (1,) * (len(dims) - 1 - dim))
    return gain


def centred(key, dims, deviation, reach, pieces=(), kind=jnp.bfloat16):
    drawn = jax.random.normal(key, dims, jnp.float32) * deviation
    if len(pieces) > 0:
        drawn = block_levels(key, dims, pieces, -0.22, 0.18) * drawn
    return jnp.clip(drawn, min=-reach, max=reach).astype(kind)


def setup_inputs(seed: int = 0) -> dict:
    key_of = jax.random.split(jax.random.key(seed), 9)
    enc_context = centred(key_of[0], (CLIPS, CAP, D_TEXT), 1.0, 6.0, ((0, 2), (1, 16), (2, 4)))
    enc_residual = draw_enc_residual(jax.random.fold_in(key_of[8], 71), 0)
    out_weight = centred(key_of[2], (D_TEXT, D_TEXT), D_TEXT ** -0.5, 0.09375, ((0, 4),))
    norm_gain = jnp.clip(1.0 + 0.18 * jax.random.normal(key_of[3], (D_TEXT,), jnp.float32), 0.1, 1.9)
    kv_weight = centred(key_of[4], (D_TEXT, 2, HEADS * HD), D_TEXT ** -0.5, 0.09375, ((2, 16),))
    caption_lengths = draw_caption_lengths(jax.random.fold_in(key_of[8], 71), 0)
    streams = draw_streams(jax.random.fold_in(key_of[8], 71), 0)
    cotangents = centred(key_of[7], (2, CLIPS, CLIP_TOK, HEADS * HD), 1.0, 6.0, ((1, 8), (2, 16)))
    return {"enc_context": enc_context, "enc_residual": enc_residual, "out_weight": out_weight, "norm_gain": norm_gain, "kv_weight": kv_weight, "caption_lengths": caption_lengths, "streams": streams, "cotangents": cotangents}


def attention_pass(query, keys, values, cotangent, valid):
    scale = 1.0 / math.sqrt(HD)
    scores = jnp.dot(query, keys.T, preferred_element_type=jnp.float32) * scale
    scores = jnp.where(valid[None, :], scores, -1e+30)
    top = lax.optimization_barrier(jnp.max(scores, axis=1, keepdims=True))
    weights = jnp.exp(scores - top)
    probs = weights / lax.optimization_barrier(jnp.sum(weights, axis=1, keepdims=True))
    rounded = probs.astype(jnp.bfloat16)
    context = jnp.dot(rounded, values, preferred_element_type=jnp.float32).astype(jnp.bfloat16)
    grad_values = jnp.dot(rounded.T, cotangent, preferred_element_type=jnp.float32).astype(jnp.bfloat16)
    grad_probs = jnp.dot(cotangent, values.T, preferred_element_type=jnp.float32)
    centre = lax.optimization_barrier(jnp.sum(probs * grad_probs, axis=1, keepdims=True))
    grad_scores = (probs * (grad_probs - centre) * scale).astype(jnp.bfloat16)
    grad_query = jnp.dot(grad_scores, keys, preferred_element_type=jnp.float32).astype(jnp.bfloat16)
    grad_keys = jnp.dot(grad_scores.T, query, preferred_element_type=jnp.float32).astype(jnp.bfloat16)
    return (context, grad_query, grad_keys, grad_values)

def split_heads(array):
    return array.reshape(array.shape[0], HEADS, HD).transpose(1, 0, 2)

def join_heads(array):
    return array.transpose(1, 0, 2).reshape(array.shape[1], HEADS * HD)

def by_heads(query, keys, values, cotangent, valid):

    def one_head(items):
        return attention_pass(items[0], items[1], items[2], items[3], valid)
    results = lax.map(one_head, (split_heads(query), split_heads(keys), split_heads(values), split_heads(cotangent)))
    return tuple((join_heads(result) for result in results))

def reference(enc_context, enc_residual, out_weight, norm_gain, kv_weight, caption_lengths, streams, cotangents):
    flat = enc_context.reshape(CLIPS * CAP, D_TEXT)
    hidden = jnp.dot(flat, out_weight, preferred_element_type=jnp.float32)
    hidden = hidden + enc_residual.reshape(CLIPS * CAP, D_TEXT).astype(jnp.float32)
    power = lax.optimization_barrier(jnp.mean(hidden * hidden, axis=1, keepdims=True))
    states = (hidden * lax.rsqrt(power + 1e-06) * norm_gain).astype(jnp.bfloat16)
    kv_flat = jnp.dot(states, kv_weight.reshape(D_TEXT, 2 * HEADS * HD), preferred_element_type=jnp.float32)
    caption_kv = kv_flat.astype(jnp.bfloat16).reshape(CLIPS, CAP, 2, HEADS * HD)
    positions = jnp.arange(CAP, dtype=jnp.int32)
    everything = jnp.arange(CLIP_TOK, dtype=jnp.int32) >= 0

    def per_clip(items):
        clip_streams, clip_cot, clip_kv, length = items
        self_parts = by_heads(clip_streams[0], clip_streams[1], clip_streams[2], clip_cot[0], everything)
        cross_parts = by_heads(clip_streams[3], clip_kv[:, 0], clip_kv[:, 1], clip_cot[1], positions < length)
        return self_parts + cross_parts
    results = lax.map(per_clip, (jnp.moveaxis(streams, 1, 0), jnp.moveaxis(cotangents, 1, 0), caption_kv, caption_lengths))
    self_ctx, self_dq, self_dk, self_dv, cross_ctx, cross_dq, cross_dk, cross_dv = results
    stream_grads = jnp.stack([self_dq, self_dk, self_dv, cross_dq])
    caption_grads = jnp.stack([cross_dk, cross_dv], axis=2).reshape(CLIPS * CAP, 2 * HEADS * HD)
    weight_grad = jnp.dot(states.T, caption_grads, preferred_element_type=jnp.float32)
    return (self_ctx, cross_ctx, stream_grads, weight_grad.reshape(D_TEXT, 2, HEADS * HD))
```

```python
import functools
import math

import jax
import jax.numpy as jnp
from jax import lax
from jax.experimental import pallas as pl
from jax.experimental.pallas import tpu as pltpu
from jax.sharding import PartitionSpec as P

D_TEXT = 4096
HD = 128
SCALE = 1.0 / math.sqrt(HD)
LOG2E = math.log2(math.e)
VMEM = 56 * 2**20

NT = (((1,), (1,)), ((), ()))
NN = (((1,), (0,)), ((), ()))
TN = (((0,), (0,)), ((), ()))


def mm(a, b, dims):
    return lax.dot_general(a, b, dims, preferred_element_type=jnp.float32)


def attend_rows(queries, keys, values, cot, valid):
    scores = mm(queries, keys, NT)
    if valid is not None:
        scores = jnp.where(valid, scores, -1e30)
    top = jnp.max(scores, axis=1, keepdims=True)
    weights = jnp.exp2((scores - top) * (SCALE * LOG2E))
    inverse = 1.0 / jnp.sum(weights, axis=1, keepdims=True)
    rounded = weights.astype(jnp.bfloat16)
    context = mm(rounded, values, NN) * inverse
    products = weights * mm(cot, values, NT)
    centre = jnp.sum(products, axis=1, keepdims=True) * inverse
    grad_scores = (products - weights * centre).astype(jnp.bfloat16)
    grad_query = mm(grad_scores, keys, NN) * (inverse * SCALE)
    cot_scaled = (cot.astype(jnp.float32) * inverse).astype(jnp.bfloat16)
    query_scaled = (queries.astype(jnp.float32) * (inverse * SCALE)).astype(jnp.bfloat16)
    return (
        context,
        grad_query,
        mm(query_scaled, grad_scores, TN),
        mm(cot_scaled, rounded, TN),
    )


def self_kernel(q_ref, k_ref, v_ref, g_ref, y_ref, dk_acc, dv_acc, *, steps, per):
    step = pl.program_id(0)
    total = k_ref.shape[0] * k_ref.shape[2]

    @pl.when(step == 0)
    def _():
        dk_acc[...] = jnp.zeros_like(dk_acc)
        dv_acc[...] = jnp.zeros_like(dv_acc)

    rows = per * k_ref.shape[2]
    for head in range(k_ref.shape[3] // HD):
        cols = slice(head * HD, (head + 1) * HD)
        context, grad_query, dk, dv = attend_rows(
            q_ref[:, 0, :, cols].reshape(rows, HD),
            k_ref[:, 0, :, cols].reshape(total, HD),
            v_ref[:, 0, :, cols].reshape(total, HD),
            g_ref[:, 0, :, cols].reshape(rows, HD),
            None,
        )
        at = pl.ds(step * per, per)
        y_ref[at, 0, :, cols] = context.astype(jnp.bfloat16).reshape(per, -1, HD)
        y_ref[at, 1, :, cols] = grad_query.astype(jnp.bfloat16).reshape(per, -1, HD)
        dk_acc[head] += dk
        dv_acc[head] += dv

    @pl.when(step == steps - 1)
    def _():
        for head in range(k_ref.shape[3] // HD):
            cols = slice(head * HD, (head + 1) * HD)
            shape = (k_ref.shape[0], k_ref.shape[2], HD)
            y_ref[:, 2, :, cols] = dk_acc[head].T.astype(jnp.bfloat16).reshape(shape)
            y_ref[:, 3, :, cols] = dv_acc[head].T.astype(jnp.bfloat16).reshape(shape)


def self_attention(x):
    blocks, _, tokens, width = x.shape
    per = max(1, 512 // tokens)
    steps = blocks // per
    heads = width // HD
    total = blocks * tokens

    def rows(which):
        return pl.BlockSpec((per, 1, tokens, width), lambda i: (i, which, 0, 0))

    def whole(which):
        return pl.BlockSpec((blocks, 1, tokens, width), lambda i: (0, which, 0, 0))

    return pl.pallas_call(
        functools.partial(self_kernel, steps=steps, per=per),
        grid=(steps,),
        in_specs=[rows(0), whole(1), whole(2), rows(3)],
        out_specs=pl.BlockSpec((blocks, 4, tokens, width), lambda i: (0, 0, 0, 0)),
        out_shape=jax.ShapeDtypeStruct(x.shape, jnp.bfloat16),
        scratch_shapes=[pltpu.VMEM((heads, HD, total), jnp.float32)] * 2,
        compiler_params=pltpu.CompilerParams(vmem_limit_bytes=VMEM),
        cost_estimate=pl.CostEstimate(
            flops=24 * heads * total * total * HD,
            bytes_accessed=4 * x.size,
            transcendentals=heads * total * total,
        ),
        name="self_attention",
    )(x, x, x, x)


def cross_kernel(len_ref, q_ref, g_ref, k_ref, v_ref, y_ref, d_ref, dk_acc, dv_acc, *, steps, per):
    step = pl.program_id(0)
    total = k_ref.shape[0]

    @pl.when(step == 0)
    def _():
        dk_acc[...] = jnp.zeros_like(dk_acc)
        dv_acc[...] = jnp.zeros_like(dv_acc)

    rows = per * q_ref.shape[2]
    heads = q_ref.shape[3] // HD
    valid = lax.broadcasted_iota(jnp.int32, (rows, total), 1) < len_ref[0]
    for head in range(heads):
        cols = slice(head * HD, (head + 1) * HD)
        context, grad_query, dk, dv = attend_rows(
            q_ref[:, 0, :, cols].reshape(rows, HD),
            k_ref[:, cols],
            v_ref[:, cols],
            g_ref[:, 0, :, cols].reshape(rows, HD),
            valid,
        )
        y_ref[:, 0, :, cols] = context.astype(jnp.bfloat16).reshape(per, -1, HD)
        y_ref[:, 1, :, cols] = grad_query.astype(jnp.bfloat16).reshape(per, -1, HD)
        dk_acc[head] += dk
        dv_acc[head] += dv

    @pl.when(step == steps - 1)
    def _():
        for head in range(heads):
            cols = slice(head * HD, (head + 1) * HD)
            d_ref[:, cols] = dk_acc[head].T.astype(jnp.bfloat16)
            cols = slice((heads + head) * HD, (heads + head + 1) * HD)
            d_ref[:, cols] = dv_acc[head].T.astype(jnp.bfloat16)


def cross_attention(lengths, x, kv):
    blocks, _, tokens, width = x.shape
    captions = kv.shape[0]
    per = max(1, 512 // tokens)
    steps = blocks // per
    heads = width // HD
    total = blocks * tokens

    def rows(which):
        return pl.BlockSpec((per, 1, tokens, width), lambda i: (i, which, 0, 0))

    return pl.pallas_call(
        functools.partial(cross_kernel, steps=steps, per=per),
        grid=(steps,),
        in_specs=[
            pl.BlockSpec(memory_space=pltpu.SMEM),
            rows(0),
            rows(1),
            pl.BlockSpec((captions, width), lambda i: (0, 0)),
            pl.BlockSpec((captions, width), lambda i: (0, 1)),
        ],
        out_specs=[
            pl.BlockSpec((per, 2, tokens, width), lambda i: (i, 0, 0, 0)),
            pl.BlockSpec((captions, 2 * width), lambda i: (0, 0)),
        ],
        out_shape=[
            jax.ShapeDtypeStruct(x.shape, jnp.bfloat16),
            jax.ShapeDtypeStruct(kv.shape, jnp.bfloat16),
        ],
        scratch_shapes=[pltpu.VMEM((heads, HD, captions), jnp.float32)] * 2,
        compiler_params=pltpu.CompilerParams(vmem_limit_bytes=VMEM),
        cost_estimate=pl.CostEstimate(
            flops=24 * heads * total * captions * HD,
            bytes_accessed=4 * x.size + 4 * kv.size,
            transcendentals=heads * total * captions,
        ),
        name="cross_attention",
    )(lengths, x, x, kv, kv)


def pack_kernel(s_ref, c_ref, x_ref):
    count = s_ref.shape[0]
    x_ref[0, :count] = s_ref[:, 0]
    x_ref[0, count:] = c_ref[:, 0]


def pack(streams, cotangents, first, count, cot, parts):
    tokens, width = streams.shape[2], streams.shape[3] // parts
    return pl.pallas_call(
        pack_kernel,
        grid=(parts,),
        in_specs=[
            pl.BlockSpec((count, 1, tokens, width), lambda j: (first // count, 0, 0, j)),
            pl.BlockSpec((1, 1, tokens, width), lambda j: (cot, 0, 0, j)),
        ],
        out_specs=pl.BlockSpec((1, count + 1, tokens, width), lambda j: (j, 0, 0, 0)),
        out_shape=jax.ShapeDtypeStruct((parts, count + 1, tokens, width), jnp.bfloat16),
        cost_estimate=pl.CostEstimate(
            flops=0, bytes_accessed=4 * (count + 1) * tokens * width * parts, transcendentals=0
        ),
        name="pack",
    )(streams, cotangents)


def unpack_kernel(a_ref, b_ref, self_ref, cross_ref, grads_ref):
    self_ref[...] = a_ref[0, 0:1]
    cross_ref[...] = b_ref[0, 0:1]
    grads_ref[0:3, 0] = a_ref[0, 1:4]
    grads_ref[3:4, 0] = b_ref[0, 1:2]


def unpack(a, b):
    parts, _, tokens, width = a.shape
    return pl.pallas_call(
        unpack_kernel,
        grid=(parts,),
        in_specs=[
            pl.BlockSpec((1, 4, tokens, width), lambda j: (j, 0, 0, 0)),
            pl.BlockSpec((1, 2, tokens, width), lambda j: (j, 0, 0, 0)),
        ],
        out_specs=[
            pl.BlockSpec((1, tokens, width), lambda j: (0, 0, j)),
            pl.BlockSpec((1, tokens, width), lambda j: (0, 0, j)),
            pl.BlockSpec((4, 1, tokens, width), lambda j: (0, 0, 0, j)),
        ],
        out_shape=[
            jax.ShapeDtypeStruct((1, tokens, parts * width), jnp.bfloat16),
            jax.ShapeDtypeStruct((1, tokens, parts * width), jnp.bfloat16),
            jax.ShapeDtypeStruct((4, 1, tokens, parts * width), jnp.bfloat16),
        ],
        cost_estimate=pl.CostEstimate(
            flops=0, bytes_accessed=4 * (a.size + b.size), transcendentals=0
        ),
        name="unpack",
    )(a, b)


def project_kernel(own_ref, x_ref, w_ref, r_ref, y_ref, *, per):
    y = mm(x_ref[...], w_ref[...], NN)
    mine = (pl.program_id(0) // per) == own_ref[0]
    y_ref[...] = y + jnp.where(mine, r_ref[...].astype(jnp.float32), 0.0)


def project(context, weight, residual):
    rows, depth = context.shape
    block = 512
    per = depth // block
    own = lax.axis_index("tp").astype(jnp.int32).reshape(1)
    return pl.pallas_call(
        functools.partial(project_kernel, per=per),
        grid=(weight.shape[1] // block,),
        in_specs=[
            pl.BlockSpec(memory_space=pltpu.SMEM),
            pl.BlockSpec((rows, depth), lambda j: (0, 0)),
            pl.BlockSpec((depth, block), lambda j: (0, j)),
            pl.BlockSpec((rows, block), lambda j: (0, lax.rem(j, per))),
        ],
        out_specs=pl.BlockSpec((rows, block), lambda j: (0, j)),
        out_shape=jax.ShapeDtypeStruct((rows, weight.shape[1]), jnp.float32),
        cost_estimate=pl.CostEstimate(
            flops=2 * rows * depth * weight.shape[1],
            bytes_accessed=2 * weight.size,
            transcendentals=0,
        ),
        name="project",
    )(own, context, weight, residual)


def body(
    enc_context,
    enc_residual,
    out_weight,
    norm_gain,
    kv_weight,
    caption_lengths,
    streams,
    cotangents,
):
    owned, caption_rows, feature_part = enc_context.shape
    parts = lax.axis_size("seq")
    local_width = kv_weight.shape[2]

    cross_in = lax.all_to_all(
        pack(streams, cotangents, 3, 1, 1, parts), "seq", split_axis=0, concat_axis=0, tiled=True
    )
    self_in = lax.all_to_all(
        pack(streams, cotangents, 0, 3, 0, parts), "seq", split_axis=0, concat_axis=0, tiled=True
    )

    partial_value = project(
        enc_context.reshape(owned * caption_rows, feature_part),
        out_weight,
        enc_residual.reshape(owned * caption_rows, feature_part),
    )
    hidden = lax.psum_scatter(partial_value, "tp", scatter_dimension=0, tiled=True)
    power = jnp.mean(hidden * hidden, axis=1, keepdims=True)
    mine = (hidden * lax.rsqrt(power + 1e-06) * norm_gain).astype(jnp.bfloat16)
    states = lax.all_gather(mine, "seq", axis=0, tiled=True)
    caption_kv = jnp.dot(
        states, kv_weight.reshape(D_TEXT, 2 * local_width), preferred_element_type=jnp.float32
    ).astype(jnp.bfloat16)

    cross_out, caption_grads = cross_attention(caption_lengths, cross_in, caption_kv)
    cross_back = lax.all_to_all(cross_out, "seq", split_axis=0, concat_axis=0, tiled=True)
    product = lax.dot_general(states, caption_grads, TN, preferred_element_type=jnp.float32)
    grad = lax.psum_scatter(
        product.astype(jnp.bfloat16), ("dp", "tp"), scatter_dimension=0, tiled=True
    )
    weight_grad = grad.astype(jnp.float32).reshape(grad.shape[0], 2, local_width)

    self_out = self_attention(self_in)
    self_back = lax.all_to_all(self_out, "seq", split_axis=0, concat_axis=0, tiled=True)
    self_ctx, cross_ctx, stream_grads = unpack(self_back, cross_back)
    return (self_ctx, cross_ctx, stream_grads, weight_grad)


def solution(mesh):
    placed = (
        P("dp", "seq", "tp"),
        P("dp", "seq", "tp"),
        P("tp", None),
        P(),
        P(None, None, "seq"),
        P(("dp", "tp")),
        P(None, ("dp", "tp"), "seq", None),
        P(None, ("dp", "tp"), "seq", None),
    )
    return jax.shard_map(
        body,
        mesh=mesh,
        in_specs=placed,
        out_specs=(
            P(("dp", "tp"), "seq", None),
            P(("dp", "tp"), "seq", None),
            P(None, ("dp", "tp"), "seq", None),
            P(("dp", "tp"), None, "seq"),
        ),
        check_vma=False,
    )
```

```python
import functools
import math

import jax
import jax.numpy as jnp
from jax import lax
from jax.experimental import pallas as pl
from jax.experimental.pallas import tpu as pltpu
from jax.sharding import PartitionSpec as P

D_TEXT = 4096
HD = 128
SCALE = 1.0 / math.sqrt(HD)
LOG2E = math.log2(math.e)
VMEM = 56 * 2**20
ADD_COST = 2 * 10**10

NT = (((1,), (1,)), ((), ()))
NN = (((1,), (0,)), ((), ()))
TN = (((0,), (0,)), ((), ()))


def mm(a, b, dims):
    return lax.dot_general(a, b, dims, preferred_element_type=jnp.float32)


def attend_rows(queries, keys, values, cot, valid):
    scores = mm(queries, keys, NT)
    if valid is not None:
        scores = jnp.where(valid, scores, -1e30)
    top = jnp.max(scores, axis=1, keepdims=True)
    weights = jnp.exp2((scores - top) * (SCALE * LOG2E))
    inverse = 1.0 / jnp.sum(weights, axis=1, keepdims=True)
    rounded = weights.astype(jnp.bfloat16)
    context = mm(rounded, values, NN) * inverse
    products = weights * mm(cot, values, NT)
    centre = jnp.sum(products, axis=1, keepdims=True) * inverse
    grad_scores = (products - weights * centre).astype(jnp.bfloat16)
    grad_query = mm(grad_scores, keys, NN) * (inverse * SCALE)
    cot_scaled = (cot.astype(jnp.float32) * inverse).astype(jnp.bfloat16)
    query_scaled = (queries.astype(jnp.float32) * (inverse * SCALE)).astype(jnp.bfloat16)
    return (
        context,
        grad_query,
        mm(query_scaled, grad_scores, TN),
        mm(cot_scaled, rounded, TN),
    )


def self_kernel(q_ref, k_ref, v_ref, g_ref, *rest, steps, per):
    y_ref, dk_acc, dv_acc = rest[-3:]
    step = pl.program_id(0)
    blocks, _, tokens, _ = k_ref.shape
    total, rows = blocks * tokens, per * tokens

    @pl.when(step == 0)
    def _():
        dk_acc[...] = jnp.zeros_like(dk_acc)
        dv_acc[...] = jnp.zeros_like(dv_acc)

    context, grad_query, dk, dv = attend_rows(
        q_ref[...].reshape(rows, HD),
        k_ref[...].reshape(total, HD),
        v_ref[...].reshape(total, HD),
        g_ref[...].reshape(rows, HD),
        None,
    )
    at = pl.ds(step * per, per)
    y_ref[at, 0] = context.astype(jnp.bfloat16).reshape(per, tokens, HD)
    y_ref[at, 1] = grad_query.astype(jnp.bfloat16).reshape(per, tokens, HD)
    dk_acc[...] += dk
    dv_acc[...] += dv

    @pl.when(step == steps - 1)
    def _():
        y_ref[:, 2] = dk_acc[...].T.astype(jnp.bfloat16).reshape(blocks, tokens, HD)
        y_ref[:, 3] = dv_acc[...].T.astype(jnp.bfloat16).reshape(blocks, tokens, HD)


def self_attention(x, head, before):
    blocks, _, tokens, _ = x.shape
    per = max(1, 512 // tokens)
    steps = blocks // per
    total = blocks * tokens

    def rows(which):
        return pl.BlockSpec((per, 1, tokens, HD), lambda i: (i, which, 0, head))

    def whole(which):
        return pl.BlockSpec((blocks, 1, tokens, HD), lambda i: (0, which, 0, head))

    earlier = [] if before is None else [before]
    return pl.pallas_call(
        functools.partial(self_kernel, steps=steps, per=per),
        grid=(steps,),
        in_specs=[rows(0), whole(1), whole(2), rows(3)]
        + [pl.BlockSpec(memory_space=pl.ANY)] * len(earlier),
        out_specs=pl.BlockSpec((blocks, 4, tokens, HD), lambda i: (0, 0, 0, head)),
        out_shape=jax.ShapeDtypeStruct(x.shape, jnp.bfloat16),
        scratch_shapes=[pltpu.VMEM((HD, total), jnp.float32)] * 2,
        input_output_aliases={4: 0} if earlier else {},
        compiler_params=pltpu.CompilerParams(vmem_limit_bytes=VMEM),
        cost_estimate=pl.CostEstimate(
            flops=24 * total * total * HD,
            bytes_accessed=16 * total * HD,
            transcendentals=total * total,
        ),
        name="self_attention",
    )(x, x, x, x, *earlier)


def cross_kernel(len_ref, pos_ref, q_ref, g_ref, k_ref, v_ref, y_ref, d_ref, dk_acc, dv_acc, *, steps, per):
    step = pl.program_id(0)
    total = k_ref.shape[0]

    @pl.when(step == 0)
    def _():
        dk_acc[...] = jnp.zeros_like(dk_acc)
        dv_acc[...] = jnp.zeros_like(dv_acc)

    rows = per * q_ref.shape[2]
    heads = q_ref.shape[3] // HD
    valid = jnp.broadcast_to(pos_ref[...], (rows, total)) < len_ref[0]
    for head in range(heads):
        cols = slice(head * HD, (head + 1) * HD)
        context, grad_query, dk, dv = attend_rows(
            q_ref[:, 0, :, cols].reshape(rows, HD),
            k_ref[:, cols],
            v_ref[:, cols],
            g_ref[:, 0, :, cols].reshape(rows, HD),
            valid,
        )
        y_ref[:, 0, :, cols] = context.astype(jnp.bfloat16).reshape(per, -1, HD)
        y_ref[:, 1, :, cols] = grad_query.astype(jnp.bfloat16).reshape(per, -1, HD)
        dk_acc[head] += dk
        dv_acc[head] += dv

    @pl.when(step == steps - 1)
    def _():
        for head in range(heads):
            cols = slice(head * HD, (head + 1) * HD)
            d_ref[:, cols] = dk_acc[head].T.astype(jnp.bfloat16)
            cols = slice((heads + head) * HD, (heads + head + 1) * HD)
            d_ref[:, cols] = dv_acc[head].T.astype(jnp.bfloat16)


def cross_attention(lengths, positions, x, kv):
    blocks, _, tokens, width = x.shape
    captions = kv.shape[0]
    per = max(1, 512 // tokens)
    steps = blocks // per
    heads = width // HD
    total = blocks * tokens

    def rows(which):
        return pl.BlockSpec((per, 1, tokens, width), lambda i: (i, which, 0, 0))

    return pl.pallas_call(
        functools.partial(cross_kernel, steps=steps, per=per),
        grid=(steps,),
        in_specs=[
            pl.BlockSpec(memory_space=pltpu.SMEM),
            pl.BlockSpec((1, captions), lambda i: (0, 0)),
            rows(0),
            rows(1),
            pl.BlockSpec((captions, width), lambda i: (0, 0)),
            pl.BlockSpec((captions, width), lambda i: (0, 1)),
        ],
        out_specs=[
            pl.BlockSpec((per, 2, tokens, width), lambda i: (i, 0, 0, 0)),
            pl.BlockSpec((captions, 2 * width), lambda i: (0, 0)),
        ],
        out_shape=[
            jax.ShapeDtypeStruct(x.shape, jnp.bfloat16),
            jax.ShapeDtypeStruct(kv.shape, jnp.bfloat16),
        ],
        scratch_shapes=[pltpu.VMEM((heads, HD, captions), jnp.float32)] * 2,
        compiler_params=pltpu.CompilerParams(vmem_limit_bytes=VMEM),
        cost_estimate=pl.CostEstimate(
            flops=24 * heads * total * captions * HD,
            bytes_accessed=4 * x.size + 4 * kv.size,
            transcendentals=heads * total * captions,
        ),
        name="cross_attention",
    )(lengths, positions.reshape(1, captions), x, x, kv, kv)


def pack_kernel(s_ref, c_ref, x_ref):
    count, width = s_ref.shape[0], x_ref.shape[3]
    for part in range(x_ref.shape[0]):
        cols = slice(part * width, (part + 1) * width)
        x_ref[part, :count] = s_ref[:, 0, :, cols]
        x_ref[part, count:] = c_ref[:, 0, :, cols]


def pack(streams, cotangents, first, count, cot, parts):
    tokens, width = streams.shape[2], streams.shape[3] // parts
    per = 4
    return pl.pallas_call(
        pack_kernel,
        grid=(parts // per,),
        in_specs=[
            pl.BlockSpec((count, 1, tokens, per * width), lambda j: (first // count, 0, 0, j)),
            pl.BlockSpec((1, 1, tokens, per * width), lambda j: (cot, 0, 0, j)),
        ],
        out_specs=pl.BlockSpec((per, count + 1, tokens, width), lambda j: (j, 0, 0, 0)),
        out_shape=jax.ShapeDtypeStruct((parts, count + 1, tokens, width), jnp.bfloat16),
        cost_estimate=pl.CostEstimate(
            flops=0, bytes_accessed=4 * (count + 1) * tokens * width * parts, transcendentals=0
        ),
        compiler_params=pltpu.CompilerParams(vmem_limit_bytes=VMEM),
        name="pack",
    )(streams, cotangents)


def unpack_self_kernel(x_ref, ctx_ref, grads_ref):
    width = x_ref.shape[3]
    for part in range(x_ref.shape[0]):
        cols = slice(part * width, (part + 1) * width)
        ctx_ref[0, :, cols] = x_ref[part, 0]
        grads_ref[:, 0, :, cols] = x_ref[part, 1:]


def unpack_self(x):
    parts, _, tokens, width = x.shape
    per = 4
    return pl.pallas_call(
        unpack_self_kernel,
        grid=(parts // per,),
        in_specs=[pl.BlockSpec((per, 4, tokens, width), lambda j: (j, 0, 0, 0))],
        out_specs=[
            pl.BlockSpec((1, tokens, per * width), lambda j: (0, 0, j)),
            pl.BlockSpec((3, 1, tokens, per * width), lambda j: (0, 0, 0, j)),
        ],
        out_shape=[
            jax.ShapeDtypeStruct((1, tokens, parts * width), jnp.bfloat16),
            jax.ShapeDtypeStruct((4, 1, tokens, parts * width), jnp.bfloat16),
        ],
        cost_estimate=pl.CostEstimate(flops=0, bytes_accessed=4 * x.size, transcendentals=0),
        compiler_params=pltpu.CompilerParams(vmem_limit_bytes=VMEM),
        name="unpack_self",
    )(x)


def unpack_cross_kernel(x_ref, _, ctx_ref, grads_ref):
    width = x_ref.shape[3]
    for part in range(x_ref.shape[0]):
        cols = slice(part * width, (part + 1) * width)
        ctx_ref[0, :, cols] = x_ref[part, 0]
        grads_ref[0, 0, :, cols] = x_ref[part, 1]


def unpack_cross(x, grads):
    parts, _, tokens, width = x.shape
    per = 4
    return pl.pallas_call(
        unpack_cross_kernel,
        grid=(parts // per,),
        in_specs=[
            pl.BlockSpec((per, 2, tokens, width), lambda j: (j, 0, 0, 0)),
            pl.BlockSpec(memory_space=pl.ANY),
        ],
        out_specs=[
            pl.BlockSpec((1, tokens, per * width), lambda j: (0, 0, j)),
            pl.BlockSpec((1, 1, tokens, per * width), lambda j: (3, 0, 0, j)),
        ],
        out_shape=[
            jax.ShapeDtypeStruct((1, tokens, parts * width), jnp.bfloat16),
            jax.ShapeDtypeStruct(grads.shape, jnp.bfloat16),
        ],
        input_output_aliases={1: 1},
        cost_estimate=pl.CostEstimate(flops=0, bytes_accessed=4 * x.size, transcendentals=0),
        compiler_params=pltpu.CompilerParams(vmem_limit_bytes=VMEM),
        name="unpack_cross",
    )(x, grads)


def project_kernel(own_ref, x_ref, w_ref, r_ref, *rest, per):
    terms, y_ref = rest[:-1], rest[-1]
    own = own_ref[0]
    y = mm(x_ref[...], w_ref[...], NN)
    mine = (pl.program_id(0) // per) == own
    y = y + jnp.where(mine, r_ref[...].astype(jnp.float32), 0.0)
    y_ref[...] = y.reshape(y_ref.shape)
    for offset, term in enumerate(terms):
        term[...] = y_ref[lax.rem(own + offset, len(terms))]


def project(context, weight, residual):
    owned, rows, depth = context.shape
    block = 512
    per = depth // block
    own = lax.axis_index("tp").astype(jnp.int32).reshape(1)
    return pl.pallas_call(
        functools.partial(project_kernel, per=per),
        grid=(weight.shape[1] // block,),
        in_specs=[
            pl.BlockSpec(memory_space=pltpu.SMEM),
            pl.BlockSpec((owned * rows, depth), lambda j: (0, 0)),
            pl.BlockSpec((depth, block), lambda j: (0, j)),
            pl.BlockSpec((owned * rows, block), lambda j: (0, lax.rem(j, per))),
        ],
        out_specs=[pl.BlockSpec((rows, block), lambda j: (0, j))] * owned,
        out_shape=[jax.ShapeDtypeStruct((rows, weight.shape[1]), jnp.float32)] * owned,
        scratch_shapes=[pltpu.VMEM((owned, rows, block), jnp.float32)],
        cost_estimate=pl.CostEstimate(
            flops=2 * owned * rows * depth * weight.shape[1],
            bytes_accessed=2 * weight.size,
            transcendentals=0,
        ),
        name="project",
    )(own, context.reshape(owned * rows, depth), weight, residual.reshape(owned * rows, depth))


def norm_kernel(*refs):
    terms, gain_ref, y_ref = refs[:-2], refs[-2], refs[-1]
    hidden = sum(term[...] for term in terms)
    power = jnp.mean(hidden * hidden, axis=1, keepdims=True)
    y = (hidden * lax.rsqrt(power + 1e-06) * gain_ref[...]).astype(jnp.bfloat16)
    for copy in range(y_ref.shape[0]):
        y_ref[copy] = y


def norm(terms, gain, copies):
    return pl.pallas_call(
        norm_kernel,
        out_shape=jax.ShapeDtypeStruct((copies,) + terms[0].shape, jnp.bfloat16),
        name="norm",
    )(*terms, gain.reshape(1, -1))


def caption_kernel(near_ref, far_ref, w_ref, kv_ref, acc):
    step = pl.program_id(0)
    half = near_ref.shape[0]
    for at, ref in ((0, near_ref), (half, far_ref)):
        terms = mm(ref[...], w_ref[...], NN)
        rows = slice(at, at + half)

        @pl.when(step == 0)
        def _():
            acc[rows] = terms

        @pl.when(step > 0)
        def _():
            acc[rows] += terms

    @pl.when(step == pl.num_programs(0) - 1)
    def _():
        kv_ref[...] = acc[...].astype(jnp.bfloat16)


def caption_projection(near, far, weight):
    half, depth = near.shape
    rows, width = 2 * half, weight.shape[1]
    block = 512
    return pl.pallas_call(
        caption_kernel,
        grid=(depth // block,),
        in_specs=[
            pl.BlockSpec((half, block), lambda j: (0, j)),
            pl.BlockSpec((half, block), lambda j: (0, j)),
            pl.BlockSpec((block, width), lambda j: (j, 0)),
        ],
        out_specs=pl.BlockSpec((rows, width), lambda j: (0, 0)),
        out_shape=jax.ShapeDtypeStruct((rows, width), jnp.bfloat16),
        scratch_shapes=[pltpu.VMEM((rows, width), jnp.float32)],
        compiler_params=pltpu.CompilerParams(vmem_limit_bytes=VMEM),
        cost_estimate=pl.CostEstimate(
            flops=2 * rows * depth * width,
            bytes_accessed=2 * rows * depth + 2 * depth * width,
            transcendentals=0,
        ),
        name="caption_projection",
    )(near, far, weight)


def split_kernel(own_ref, x_ref, *outs):
    block = x_ref.shape[1] // len(outs)
    for clip in range(len(outs)):
        for offset, out in enumerate(outs):

            @pl.when(lax.rem(own_ref[0] + offset, len(outs)) == clip)
            def _():
                out[...] = x_ref[:, clip * block : (clip + 1) * block]


def split_features(rows, groups, clips):
    count, depth = rows.shape
    own = lax.axis_index("tp").astype(jnp.int32).reshape(1)
    return pl.pallas_call(
        split_kernel,
        grid=(groups,),
        in_specs=[
            pl.BlockSpec(memory_space=pltpu.SMEM),
            pl.BlockSpec((count, depth // groups), lambda d: (0, d)),
        ],
        out_specs=[pl.BlockSpec((count, depth // (groups * clips)), lambda d: (0, d))] * clips,
        out_shape=[jax.ShapeDtypeStruct((count, depth // clips), rows.dtype)] * clips,
        cost_estimate=pl.CostEstimate(
            flops=0, bytes_accessed=4 * rows.size, transcendentals=0
        ),
        name="split_features",
    )(own, rows)


def weight_kernel(own_ref, *refs, clips):
    near, far, grads = refs[:clips], refs[clips : 2 * clips], refs[2 * clips : 3 * clips]
    kept_ref, sent_ref = refs[-2:]
    half = near[0].shape[0]
    total = sum(
        mm(x[...], g[:half], TN) + mm(y[...], g[half:], TN) for x, y, g in zip(near, far, grads)
    )
    mine = pl.program_id(0) == own_ref[0]

    @pl.when(mine)
    def _():
        kept_ref[...] = total

    @pl.when(jnp.logical_not(mine))
    def _():
        sent_ref[...] = total.astype(jnp.bfloat16)


def weight_terms(near, far, grads, groups):
    clips = len(near)
    rows, width = grads[0].shape
    block = near[0].shape[1] // groups
    own = lax.axis_index("dp").astype(jnp.int32).reshape(1)
    return pl.pallas_call(
        functools.partial(weight_kernel, clips=clips),
        grid=(groups,),
        in_specs=[pl.BlockSpec(memory_space=pltpu.SMEM)]
        + [pl.BlockSpec((rows // 2, block), lambda d: (0, d))] * (2 * clips)
        + [pl.BlockSpec((rows, width), lambda d: (0, 0))] * clips,
        out_specs=[pl.BlockSpec((block, width), lambda d: (0, 0))] * 2,
        out_shape=[
            jax.ShapeDtypeStruct((block, width), jnp.float32),
            jax.ShapeDtypeStruct((block, width), jnp.bfloat16),
        ],
        compiler_params=pltpu.CompilerParams(vmem_limit_bytes=VMEM),
        cost_estimate=pl.CostEstimate(
            flops=2 * clips * groups * rows * block * width,
            bytes_accessed=2 * clips * rows * (groups * block + width),
            transcendentals=0,
        ),
        name="weight_terms",
    )(own, *near, *far, *grads)


def add_kernel(kept_ref, taken_ref, y_ref):
    y_ref[...] = kept_ref[...] + taken_ref[...].astype(jnp.float32)


def add_taken(kept, taken):
    rows, width = kept.shape
    block = pl.BlockSpec((rows // 4, width), lambda j: (j, 0))
    return pl.pallas_call(
        add_kernel,
        grid=(4,),
        in_specs=[block, block],
        out_specs=block,
        out_shape=jax.ShapeDtypeStruct(kept.shape, jnp.float32),
        cost_estimate=pl.CostEstimate(
            flops=ADD_COST, bytes_accessed=10 * kept.size, transcendentals=0
        ),
        name="add_taken",
    )(kept, taken)


def shifts(size, offset):
    return [(at, (at + offset) % size) for at in range(size)]


def seq_exchange(x):
    return lax.all_to_all(x, "seq", split_axis=0, concat_axis=0, tiled=True)


def tp_terms(terms):
    size = len(terms)
    return [terms[0]] + [
        lax.ppermute(terms[offset], "tp", shifts(size, offset)) for offset in range(1, size)
    ]


CORES = 2


def gather_captions(copies):
    size = lax.axis_size("seq")
    groups = [list(range(core, size, CORES)) for core in range(CORES)]
    rows = lax.all_to_all(
        copies, "seq", split_axis=0, concat_axis=0, tiled=True, axis_index_groups=groups
    )
    return rows.reshape(-1, copies.shape[2])


def other_core(x):
    size = lax.axis_size("seq")
    return lax.ppermute(x, "seq", [(source, source ^ 1) for source in range(size)])


def caption_order(rows):
    size, core = lax.axis_size("seq"), lax.axis_index("seq") % CORES
    chips = jnp.arange(0, size, CORES, dtype=jnp.int32)
    places = jnp.concatenate([chips + core, chips + (1 - core)])
    return (places[:, None] * rows + jnp.arange(rows, dtype=jnp.int32)[None, :]).reshape(-1)


def body(
    enc_context,
    enc_residual,
    out_weight,
    norm_gain,
    kv_weight,
    caption_lengths,
    streams,
    cotangents,
):
    parts = lax.axis_size("seq")
    groups, clips = lax.axis_size("dp"), lax.axis_size("tp")
    local_width = kv_weight.shape[2]

    self_packed = pack(streams, cotangents, 0, 3, 0, parts)
    self_in = seq_exchange(self_packed)
    streams, cotangents, enc_context, _ = lax.optimization_barrier(
        (streams, cotangents, enc_context, self_packed)
    )
    terms = tp_terms(project(enc_context, out_weight, enc_residual))
    cross_packed = pack(streams, cotangents, 3, 1, 1, parts)
    kv_flat = kv_weight.reshape(kv_weight.shape[0], 2 * local_width)
    terms, kv_flat, cross_packed, _ = lax.optimization_barrier(
        (terms, kv_flat, cross_packed, self_in)
    )
    near = gather_captions(norm(terms, norm_gain, parts // CORES))
    self_out = None
    for head in range(local_width // HD):
        self_out = self_attention(self_in, head, self_out)

    near, cross_packed, _ = lax.optimization_barrier((near, cross_packed, self_out))
    cross_in = seq_exchange(cross_packed)
    far = other_core(near)
    near_terms = tp_terms(split_features(near, groups, clips))
    caption_kv = caption_projection(near, far, kv_flat)

    self_out, _, _, near_terms = lax.optimization_barrier(
        (self_out, cross_in, caption_kv, near_terms)
    )
    self_back = seq_exchange(self_out)
    far_terms = [other_core(x) for x in near_terms]
    order = caption_order(enc_context.shape[1])
    cross_out, caption_grads = cross_attention(caption_lengths, order, cross_in, caption_kv)
    caption_grads, far_terms = lax.optimization_barrier((caption_grads, far_terms))
    grads = tp_terms([caption_grads] * clips)
    kept, sent = weight_terms(near_terms, far_terms, grads, groups)

    cross_out, _, _ = lax.optimization_barrier((cross_out, self_back, sent))
    cross_back = seq_exchange(cross_out)
    self_ctx, stream_grads = unpack_self(self_back)
    taken = lax.ppermute(sent, "dp", shifts(groups, 1))
    kept, _ = lax.optimization_barrier((kept, self_ctx))
    grad = add_taken(kept, taken)
    weight_grad = grad.reshape(grad.shape[0], 2, local_width)
    cross_ctx, stream_grads = unpack_cross(cross_back, stream_grads)
    return (self_ctx, cross_ctx, stream_grads, weight_grad)


def solution(mesh):
    placed = (
        P("dp", "seq", "tp"),
        P("dp", "seq", "tp"),
        P("tp", None),
        P(),
        P(None, None, "seq"),
        P(("dp", "tp")),
        P(None, ("dp", "tp"), "seq", None),
        P(None, ("dp", "tp"), "seq", None),
    )
    return jax.shard_map(
        body,
        mesh=mesh,
        in_specs=placed,
        out_specs=(
            P(("dp", "tp"), "seq", None),
            P(("dp", "tp"), "seq", None),
            P(None, ("dp", "tp"), "seq", None),
            P(("dp", "tp"), None, "seq"),
        ),
        check_vma=False,
    )
```

```python
import functools
import math

import jax
import jax.numpy as jnp
from jax import lax
from jax.experimental import pallas as pl
from jax.experimental.pallas import tpu as pltpu
from jax.sharding import PartitionSpec as P

D_TEXT = 4096
HD = 128
SCALE = 1.0 / math.sqrt(HD)
LOG2E = math.log2(math.e)
VMEM = 56 * 2**20
SMALL = 12 * 2**20
MIDDLE = 28 * 2**20
VMEM_SELF = 36 * 2**20
ADD_COST = 2 * 10**10
CROSS_COST = 6 * 10**9
CORES = 2

NT = (((1,), (1,)), ((), ()))
NN = (((1,), (0,)), ((), ()))
TN = (((0,), (0,)), ((), ()))


def mm(a, b, dims):
    return lax.dot_general(a, b, dims, preferred_element_type=jnp.float32)


def attend_rows(queries, keys, values, cot, valid):
    scores = mm(queries, keys, NT)
    if valid is not None:
        scores = jnp.where(valid, scores, -1e30)
    top = jnp.max(scores, axis=1, keepdims=True)
    weights = jnp.exp2((scores - top) * (SCALE * LOG2E))
    inverse = 1.0 / jnp.sum(weights, axis=1, keepdims=True)
    rounded = weights.astype(jnp.bfloat16)
    context = mm(rounded, values, NN) * inverse
    products = weights * mm(cot, values, NT)
    centre = jnp.sum(products, axis=1, keepdims=True) * inverse
    grad_scores = (products - weights * centre).astype(jnp.bfloat16)
    grad_query = mm(grad_scores, keys, NN) * (inverse * SCALE)
    cot_scaled = (cot.astype(jnp.float32) * inverse).astype(jnp.bfloat16)
    query_scaled = (queries.astype(jnp.float32) * (inverse * SCALE)).astype(jnp.bfloat16)
    return (
        context,
        grad_query,
        mm(query_scaled, grad_scores, TN),
        mm(cot_scaled, rounded, TN),
    )


def self_kernel(q_ref, k_ref, v_ref, g_ref, *rest, steps, per):
    y_ref, dk_acc, dv_acc = rest[-3:]
    step = pl.program_id(0)
    blocks, _, tokens, _ = k_ref.shape
    total, rows = blocks * tokens, per * tokens

    @pl.when(step == 0)
    def _():
        dk_acc[...] = jnp.zeros_like(dk_acc)
        dv_acc[...] = jnp.zeros_like(dv_acc)

    context, grad_query, dk, dv = attend_rows(
        q_ref[...].reshape(rows, HD),
        k_ref[...].reshape(total, HD),
        v_ref[...].reshape(total, HD),
        g_ref[...].reshape(rows, HD),
        None,
    )
    at = pl.ds(step * per, per)
    y_ref[at, 0] = context.astype(jnp.bfloat16).reshape(per, tokens, HD)
    y_ref[at, 1] = grad_query.astype(jnp.bfloat16).reshape(per, tokens, HD)
    dk_acc[...] += dk
    dv_acc[...] += dv

    @pl.when(step == steps - 1)
    def _():
        y_ref[:, 2] = dk_acc[...].T.astype(jnp.bfloat16).reshape(blocks, tokens, HD)
        y_ref[:, 3] = dv_acc[...].T.astype(jnp.bfloat16).reshape(blocks, tokens, HD)


def self_attention(x, head, before):
    blocks, _, tokens, _ = x.shape
    per = max(1, 512 // tokens)
    steps = blocks // per
    total = blocks * tokens

    def rows(which):
        return pl.BlockSpec((per, 1, tokens, HD), lambda i: (i, which, 0, head))

    def whole(which):
        return pl.BlockSpec((blocks, 1, tokens, HD), lambda i: (0, which, 0, head))

    earlier = [] if before is None else [before]
    return pl.pallas_call(
        functools.partial(self_kernel, steps=steps, per=per),
        grid=(steps,),
        in_specs=[rows(0), whole(1), whole(2), rows(3)]
        + [pl.BlockSpec(memory_space=pl.ANY)] * len(earlier),
        out_specs=pl.BlockSpec((blocks, 4, tokens, HD), lambda i: (0, 0, 0, head)),
        out_shape=jax.ShapeDtypeStruct(x.shape, jnp.bfloat16),
        scratch_shapes=[pltpu.VMEM((HD, total), jnp.float32)] * 2,
        input_output_aliases={4: 0} if earlier else {},
        compiler_params=pltpu.CompilerParams(vmem_limit_bytes=VMEM_SELF),
        cost_estimate=pl.CostEstimate(
            flops=24 * total * total * HD,
            bytes_accessed=16 * total * HD,
            transcendentals=total * total,
        ),
        name="self_attention",
    )(x, x, x, x, *earlier)


def cross_kernel(core_ref, len_ref, pos_ref, x_ref, k_ref, v_ref, y_ref, d_ref, dk_acc, dv_acc):
    step = pl.program_id(0)
    total = k_ref.shape[0]

    @pl.when(step == 0)
    def _():
        dk_acc[...] = jnp.zeros_like(dk_acc)
        dv_acc[...] = jnp.zeros_like(dv_acc)

    chips, _, tokens, width = x_ref.shape
    rows = chips * CORES * tokens
    heads = width // HD
    valid = jnp.broadcast_to(pos_ref[...], (rows, total)) < len_ref[0]
    for head in range(heads):
        cols = slice(head * HD, (head + 1) * HD)
        context, grad_query, dk, dv = attend_rows(
            jnp.concatenate([x_ref[:, 0, :, cols], x_ref[:, 2, :, cols]]).reshape(rows, HD),
            k_ref[:, cols],
            v_ref[:, cols],
            jnp.concatenate([x_ref[:, 1, :, cols], x_ref[:, 3, :, cols]]).reshape(rows, HD),
            valid,
        )
        shape = (CORES, chips, tokens, HD)
        context = context.astype(jnp.bfloat16).reshape(shape)
        grad_query = grad_query.astype(jnp.bfloat16).reshape(shape)
        for chip in range(chips):
            for other in range(CORES):
                at = CORES * chip + lax.rem(core_ref[0] + other, CORES)
                y_ref[at, 0, :, cols] = context[other, chip]
                y_ref[at, 1, :, cols] = grad_query[other, chip]
        dk_acc[head] += dk
        dv_acc[head] += dv

    @pl.when(step == pl.num_programs(0) - 1)
    def _():
        for head in range(heads):
            cols = slice(head * HD, (head + 1) * HD)
            d_ref[:, cols] = dk_acc[head].T.astype(jnp.bfloat16)
            cols = slice((heads + head) * HD, (heads + head + 1) * HD)
            d_ref[:, cols] = dv_acc[head].T.astype(jnp.bfloat16)


def cross_attention(core, lengths, positions, x, kv):
    chips, _, tokens, width = x.shape
    captions = kv.shape[0]
    per = max(1, 512 // (CORES * tokens))
    heads = width // HD
    total = chips * CORES * tokens
    return pl.pallas_call(
        cross_kernel,
        grid=(chips // per,),
        in_specs=[
            pl.BlockSpec(memory_space=pltpu.SMEM),
            pl.BlockSpec(memory_space=pltpu.SMEM),
            pl.BlockSpec((1, captions), lambda i: (0, 0)),
            pl.BlockSpec((per, 2 * CORES, tokens, width), lambda i: (i, 0, 0, 0)),
            pl.BlockSpec((captions, width), lambda i: (0, 0)),
            pl.BlockSpec((captions, width), lambda i: (0, 1)),
        ],
        out_specs=[
            pl.BlockSpec((CORES * per, 2, tokens, width), lambda i: (i, 0, 0, 0)),
            pl.BlockSpec((captions, 2 * width), lambda i: (0, 0)),
        ],
        out_shape=[
            jax.ShapeDtypeStruct((CORES * chips, 2, tokens, width), jnp.bfloat16),
            jax.ShapeDtypeStruct(kv.shape, jnp.bfloat16),
        ],
        scratch_shapes=[pltpu.VMEM((heads, HD, captions), jnp.float32)] * 2,
        compiler_params=pltpu.CompilerParams(vmem_limit_bytes=MIDDLE),
        cost_estimate=pl.CostEstimate(
            flops=CROSS_COST,
            bytes_accessed=8 * total * width + 4 * kv.size,
            transcendentals=heads * total * captions,
        ),
        name="cross_attention",
    )(core, lengths, positions.reshape(1, captions), x, kv, kv)


def pack_kernel(s_ref, c_ref, x_ref):
    count, width = s_ref.shape[0], x_ref.shape[3]
    for part in range(x_ref.shape[0]):
        cols = slice(part * width, (part + 1) * width)
        x_ref[part, :count] = s_ref[:, 0, :, cols]
        x_ref[part, count:] = c_ref[:, 0, :, cols]


def pack(streams, cotangents, first, count, cot, parts):
    tokens, width = streams.shape[2], streams.shape[3] // parts
    per = 4
    return pl.pallas_call(
        pack_kernel,
        grid=(parts // per,),
        in_specs=[
            pl.BlockSpec((count, 1, tokens, per * width), lambda j: (first // count, 0, 0, j)),
            pl.BlockSpec((1, 1, tokens, per * width), lambda j: (cot, 0, 0, j)),
        ],
        out_specs=pl.BlockSpec((per, count + 1, tokens, width), lambda j: (j, 0, 0, 0)),
        out_shape=jax.ShapeDtypeStruct((parts, count + 1, tokens, width), jnp.bfloat16),
        cost_estimate=pl.CostEstimate(
            flops=0, bytes_accessed=4 * (count + 1) * tokens * width * parts, transcendentals=0
        ),
        compiler_params=pltpu.CompilerParams(vmem_limit_bytes=VMEM),
        name="pack",
    )(streams, cotangents)


def pack_cores_kernel(core_ref, s_ref, c_ref, keep_ref, give_ref):
    width = keep_ref.shape[3]
    for core in range(CORES):
        cols = slice(core * width, (core + 1) * width)

        @pl.when(core_ref[0] == core)
        def _():
            keep_ref[0, 0] = s_ref[0, 0, :, cols]
            keep_ref[0, 1] = c_ref[0, 0, :, cols]

        @pl.when(core_ref[0] != core)
        def _():
            give_ref[0, 0] = s_ref[0, 0, :, cols]
            give_ref[0, 1] = c_ref[0, 0, :, cols]


def pack_cores(core, streams, cotangents, stream, cot, parts):
    tokens, width = streams.shape[2], streams.shape[3] // parts
    chips = parts // CORES
    slab = pl.BlockSpec((1, 2, tokens, width), lambda j: (j, 0, 0, 0))
    return pl.pallas_call(
        pack_cores_kernel,
        grid=(chips,),
        in_specs=[
            pl.BlockSpec(memory_space=pltpu.SMEM),
            pl.BlockSpec((1, 1, tokens, CORES * width), lambda j: (stream, 0, 0, j)),
            pl.BlockSpec((1, 1, tokens, CORES * width), lambda j: (cot, 0, 0, j)),
        ],
        out_specs=[slab, slab],
        out_shape=[jax.ShapeDtypeStruct((chips, 2, tokens, width), jnp.bfloat16)] * 2,
        compiler_params=pltpu.CompilerParams(vmem_limit_bytes=VMEM),
        cost_estimate=pl.CostEstimate(
            flops=0, bytes_accessed=8 * tokens * width * parts, transcendentals=0
        ),
        name="pack_cores",
    )(core, streams, cotangents)


def unpack_self_kernel(x_ref, ctx_ref, grads_ref):
    width = x_ref.shape[3]
    for part in range(x_ref.shape[0]):
        cols = slice(part * width, (part + 1) * width)
        ctx_ref[0, :, cols] = x_ref[part, 0]
        grads_ref[:, 0, :, cols] = x_ref[part, 1:]


def unpack_self(x):
    parts, _, tokens, width = x.shape
    per = 4
    return pl.pallas_call(
        unpack_self_kernel,
        grid=(parts // per,),
        in_specs=[pl.BlockSpec((per, 4, tokens, width), lambda j: (j, 0, 0, 0))],
        out_specs=[
            pl.BlockSpec((1, tokens, per * width), lambda j: (0, 0, j)),
            pl.BlockSpec((3, 1, tokens, per * width), lambda j: (0, 0, 0, j)),
        ],
        out_shape=[
            jax.ShapeDtypeStruct((1, tokens, parts * width), jnp.bfloat16),
            jax.ShapeDtypeStruct((4, 1, tokens, parts * width), jnp.bfloat16),
        ],
        cost_estimate=pl.CostEstimate(flops=0, bytes_accessed=4 * x.size, transcendentals=0),
        compiler_params=pltpu.CompilerParams(vmem_limit_bytes=SMALL),
        name="unpack_self",
    )(x)


def unpack_cross_kernel(x_ref, _, ctx_ref, grads_ref):
    width = x_ref.shape[3]
    for part in range(x_ref.shape[0]):
        cols = slice(part * width, (part + 1) * width)
        ctx_ref[0, :, cols] = x_ref[part, 0]
        grads_ref[0, 0, :, cols] = x_ref[part, 1]


def unpack_cross(x, grads):
    parts, _, tokens, width = x.shape
    per = 4
    return pl.pallas_call(
        unpack_cross_kernel,
        grid=(parts // per,),
        in_specs=[
            pl.BlockSpec((per, 2, tokens, width), lambda j: (j, 0, 0, 0)),
            pl.BlockSpec(memory_space=pl.ANY),
        ],
        out_specs=[
            pl.BlockSpec((1, tokens, per * width), lambda j: (0, 0, j)),
            pl.BlockSpec((1, 1, tokens, per * width), lambda j: (3, 0, 0, j)),
        ],
        out_shape=[
            jax.ShapeDtypeStruct((1, tokens, parts * width), jnp.bfloat16),
            jax.ShapeDtypeStruct(grads.shape, jnp.bfloat16),
        ],
        input_output_aliases={1: 1},
        cost_estimate=pl.CostEstimate(flops=0, bytes_accessed=4 * x.size, transcendentals=0),
        compiler_params=pltpu.CompilerParams(vmem_limit_bytes=SMALL),
        name="unpack_cross",
    )(x, grads)


def project_kernel(own_ref, x_ref, w_ref, r_ref, *rest, per):
    terms, y_ref = rest[:-1], rest[-1]
    own = own_ref[0]
    y = mm(x_ref[...], w_ref[...], NN)
    mine = (pl.program_id(0) // per) == own
    y = y + jnp.where(mine, r_ref[...].astype(jnp.float32), 0.0)
    y_ref[...] = y.reshape(y_ref.shape)
    for offset, term in enumerate(terms):
        term[...] = y_ref[lax.rem(own + offset, len(terms))]


def project(context, weight, residual):
    owned, rows, depth = context.shape
    block = 512
    per = depth // block
    own = lax.axis_index("tp").astype(jnp.int32).reshape(1)
    return pl.pallas_call(
        functools.partial(project_kernel, per=per),
        grid=(weight.shape[1] // block,),
        in_specs=[
            pl.BlockSpec(memory_space=pltpu.SMEM),
            pl.BlockSpec((owned * rows, depth), lambda j: (0, 0)),
            pl.BlockSpec((depth, block), lambda j: (0, j)),
            pl.BlockSpec((owned * rows, block), lambda j: (0, lax.rem(j, per))),
        ],
        out_specs=[pl.BlockSpec((rows, block), lambda j: (0, j))] * owned,
        out_shape=[jax.ShapeDtypeStruct((rows, weight.shape[1]), jnp.float32)] * owned,
        scratch_shapes=[pltpu.VMEM((owned, rows, block), jnp.float32)],
        cost_estimate=pl.CostEstimate(
            flops=2 * owned * rows * depth * weight.shape[1],
            bytes_accessed=2 * weight.size,
            transcendentals=0,
        ),
        name="project",
    )(own, context.reshape(owned * rows, depth), weight, residual.reshape(owned * rows, depth))


def join_kernel(own_ref, other_ref, y_ref):
    y_ref[:, :2] = own_ref[...]
    y_ref[:, 2:] = other_ref[...]


def join_cores(own, other, blocks):
    chips, count, tokens, width = own.shape
    per = 2
    slab = pl.BlockSpec((per, count, tokens, width), lambda j: (j, 0, 0, 0))
    return pl.pallas_call(
        join_kernel,
        grid=(chips // per,),
        in_specs=[slab, slab],
        out_specs=pl.BlockSpec((per, 2 * count, tokens, width), lambda j: (j, 0, 0, 0)),
        out_shape=jax.ShapeDtypeStruct((chips, 2 * count + blocks, tokens, width), jnp.bfloat16),
        compiler_params=pltpu.CompilerParams(vmem_limit_bytes=SMALL),
        name="join_cores",
    )(own, other)


def norm_kernel(*refs):
    terms, (gain_ref, _, y_ref, states) = refs[:-4], refs[-4:]
    blocks, rows, width = states.shape

    @pl.when(pl.program_id(0) == 0)
    def _():
        hidden = sum(term[...] for term in terms)
        power = jnp.mean(hidden * hidden, axis=1, keepdims=True)
        normed = (hidden * lax.rsqrt(power + 1e-06) * gain_ref[...]).astype(jnp.bfloat16)
        held = terms[0].shape[0]
        per = rows // held
        for at in range(blocks * per):
            to = pl.ds(at % per * held, held)
            states[at // per, to] = normed[:, at * width : (at + 1) * width]

    for chip in range(y_ref.shape[0]):
        y_ref[chip] = states[...]


def norm_into(terms, gain, packed, blocks):
    chips, total, tokens, width = packed.shape
    rows, depth = terms[0].shape
    per = 2
    return pl.pallas_call(
        norm_kernel,
        grid=(chips // per,),
        in_specs=[pl.BlockSpec((rows, depth), lambda j: (0, 0))] * len(terms)
        + [pl.BlockSpec((1, depth), lambda j: (0, 0)), pl.BlockSpec(memory_space=pl.ANY)],
        out_specs=pl.BlockSpec(
            (per, blocks, tokens, width), lambda j: (j, total // blocks - 1, 0, 0)
        ),
        out_shape=jax.ShapeDtypeStruct(packed.shape, jnp.bfloat16),
        scratch_shapes=[pltpu.VMEM((blocks, tokens, width), jnp.bfloat16)],
        input_output_aliases={len(terms) + 1: 0},
        compiler_params=pltpu.CompilerParams(vmem_limit_bytes=SMALL),
        name="norm_into",
    )(*terms, gain.reshape(1, -1), packed)


def caption_kernel(near_ref, far_ref, w_ref, kv_ref, acc, *, held):
    step = pl.program_id(0)
    chips, _, rows, width = near_ref.shape
    half = chips * held
    for at, ref in ((0, near_ref), (half, far_ref)):
        terms = sum(
            mm(
                ref[:, 0, block * held : (block + 1) * held].reshape(half, width),
                w_ref[block * width : (block + 1) * width],
                NN,
            )
            for block in range(rows // held)
        )
        to = slice(at, at + half)

        @pl.when(step == 0)
        def _():
            acc[to] = terms

        @pl.when(step > 0)
        def _():
            acc[to] += terms

    @pl.when(step == pl.num_programs(0) - 1)
    def _():
        kv_ref[...] = acc[...].astype(jnp.bfloat16)


def caption_projection(near, skip, far, weight, held):
    chips, blocks, rows, columns = far.shape
    blocks -= skip
    captions, width = CORES * chips * held, weight.shape[1]
    depth = columns * rows // held
    return pl.pallas_call(
        functools.partial(caption_kernel, held=held),
        grid=(blocks,),
        in_specs=[
            pl.BlockSpec((chips, 1, rows, columns), lambda j: (0, skip + j, 0, 0)),
            pl.BlockSpec((chips, 1, rows, columns), lambda j: (0, skip + j, 0, 0)),
            pl.BlockSpec((depth, width), lambda j: (j, 0)),
        ],
        out_specs=pl.BlockSpec((captions, width), lambda j: (0, 0)),
        out_shape=jax.ShapeDtypeStruct((captions, width), jnp.bfloat16),
        scratch_shapes=[pltpu.VMEM((captions, width), jnp.float32)],
        compiler_params=pltpu.CompilerParams(vmem_limit_bytes=MIDDLE),
        cost_estimate=pl.CostEstimate(
            flops=2 * captions * blocks * depth * width,
            bytes_accessed=4 * far.size + 2 * weight.size,
            transcendentals=0,
        ),
        name="caption_projection",
    )(near, far, weight)


def split_kernel(own_ref, x_ref, *outs, held):
    chips, blocks, rows, columns = x_ref.shape
    per = rows // held
    count = blocks * per // len(outs)
    for clip in range(len(outs)):
        for offset, out in enumerate(outs):

            @pl.when(lax.rem(own_ref[0] + offset, len(outs)) == clip)
            def _():
                for at in range(count):
                    block, place = divmod(clip * count + at, per)
                    piece = x_ref[:, block, place * held : (place + 1) * held]
                    out[:, at * columns : (at + 1) * columns] = piece.reshape(-1, columns)


def split_features(x, skip, groups, clips, held):
    chips, blocks, rows, columns = x.shape
    blocks = (blocks - skip) // groups
    depth = blocks * columns * rows // held // clips
    own = lax.axis_index("tp").astype(jnp.int32).reshape(1)
    return pl.pallas_call(
        functools.partial(split_kernel, held=held),
        grid=(groups,),
        in_specs=[
            pl.BlockSpec(memory_space=pltpu.SMEM),
            pl.BlockSpec((chips, blocks, rows, columns), lambda d: (0, skip // blocks + d, 0, 0)),
        ],
        out_specs=[pl.BlockSpec((chips * held, depth), lambda d: (0, d))] * clips,
        out_shape=[jax.ShapeDtypeStruct((chips * held, groups * depth), x.dtype)] * clips,
        compiler_params=pltpu.CompilerParams(vmem_limit_bytes=SMALL),
        cost_estimate=pl.CostEstimate(
            flops=0, bytes_accessed=2 * x.size, transcendentals=0
        ),
        name="split_features",
    )(own, x)


def weight_kernel(own_ref, *refs, clips):
    near, far, grads = refs[:clips], refs[clips : 2 * clips], refs[2 * clips : 3 * clips]
    kept_ref, sent_ref = refs[-2:]
    half = near[0].shape[0]
    total = sum(
        mm(x[...], g[:half], TN) + mm(y[...], g[half:], TN) for x, y, g in zip(near, far, grads)
    )
    mine = pl.program_id(0) == own_ref[0]

    @pl.when(mine)
    def _():
        kept_ref[...] = total

    @pl.when(jnp.logical_not(mine))
    def _():
        sent_ref[...] = total.astype(jnp.bfloat16)


def weight_terms(near, far, grads, groups):
    clips = len(near)
    rows, width = grads[0].shape
    block = near[0].shape[1] // groups
    own = lax.axis_index("dp").astype(jnp.int32).reshape(1)
    return pl.pallas_call(
        functools.partial(weight_kernel, clips=clips),
        grid=(groups,),
        in_specs=[pl.BlockSpec(memory_space=pltpu.SMEM)]
        + [pl.BlockSpec((rows // 2, block), lambda d: (0, d))] * (2 * clips)
        + [pl.BlockSpec((rows, width), lambda d: (0, 0))] * clips,
        out_specs=[pl.BlockSpec((block, width), lambda d: (0, 0))] * 2,
        out_shape=[
            jax.ShapeDtypeStruct((block, width), jnp.float32),
            jax.ShapeDtypeStruct((block, width), jnp.bfloat16),
        ],
        compiler_params=pltpu.CompilerParams(vmem_limit_bytes=MIDDLE),
        cost_estimate=pl.CostEstimate(
            flops=2 * clips * groups * rows * block * width,
            bytes_accessed=2 * clips * rows * (groups * block + width),
            transcendentals=0,
        ),
        name="weight_terms",
    )(own, *near, *far, *grads)


def add_kernel(kept_ref, taken_ref, y_ref):
    y_ref[...] = kept_ref[...] + taken_ref[...].astype(jnp.float32)


def add_taken(kept, taken):
    rows, width = kept.shape
    block = pl.BlockSpec((rows // 4, width), lambda j: (j, 0))
    return pl.pallas_call(
        add_kernel,
        grid=(4,),
        in_specs=[block, block],
        out_specs=block,
        out_shape=jax.ShapeDtypeStruct(kept.shape, jnp.float32),
        cost_estimate=pl.CostEstimate(
            flops=ADD_COST, bytes_accessed=10 * kept.size, transcendentals=0
        ),
        name="add_taken",
    )(kept, taken)


def shifts(size, offset):
    return [(at, (at + offset) % size) for at in range(size)]


def seq_exchange(x):
    return lax.all_to_all(x, "seq", split_axis=0, concat_axis=0, tiled=True)


def tp_terms(terms):
    size = len(terms)
    return [terms[0]] + [
        lax.ppermute(terms[offset], "tp", shifts(size, offset)) for offset in range(1, size)
    ]


def core_exchange(x):
    size = lax.axis_size("seq")
    groups = [list(range(core, size, CORES)) for core in range(CORES)]
    return lax.all_to_all(
        x, "seq", split_axis=0, concat_axis=0, tiled=True, axis_index_groups=groups
    )


def other_core(x):
    size = lax.axis_size("seq")
    return lax.ppermute(x, "seq", [(source, source ^ 1) for source in range(size)])


def caption_order(rows):
    size, core = lax.axis_size("seq"), lax.axis_index("seq") % CORES
    chips = jnp.arange(0, size, CORES, dtype=jnp.int32)
    places = jnp.concatenate([chips + core, chips + (1 - core)])
    return (places[:, None] * rows + jnp.arange(rows, dtype=jnp.int32)[None, :]).reshape(-1)


def body(
    enc_context,
    enc_residual,
    out_weight,
    norm_gain,
    kv_weight,
    caption_lengths,
    streams,
    cotangents,
):
    parts = lax.axis_size("seq")
    groups, clips = lax.axis_size("dp"), lax.axis_size("tp")
    local_width = kv_weight.shape[2]

    held = enc_context.shape[1]
    core = (lax.axis_index("seq") % CORES).astype(jnp.int32).reshape(1)

    self_packed = pack(streams, cotangents, 0, 3, 0, parts)
    self_in = seq_exchange(self_packed)
    streams, cotangents, enc_context, _ = lax.optimization_barrier(
        (streams, cotangents, enc_context, self_packed)
    )
    terms = tp_terms(project(enc_context, out_weight, enc_residual))
    keep, give = pack_cores(core, streams, cotangents, 3, 1, parts)
    blocks = terms[0].size // (keep.shape[2] * keep.shape[3])
    packed = join_cores(keep, other_core(give), blocks)
    kv_flat = kv_weight.reshape(kv_weight.shape[0], 2 * local_width)
    packed, kv_flat, _ = lax.optimization_barrier(
        (norm_into(terms, norm_gain, packed, blocks), kv_flat, self_in)
    )
    mixed = core_exchange(packed)
    self_out = None
    for head in range(local_width // HD):
        self_out = self_attention(self_in, head, self_out)

    self_out, mixed = lax.optimization_barrier((self_out, mixed))
    self_back = seq_exchange(self_out)
    skip = 2 * CORES
    near_terms = tp_terms(split_features(mixed, skip, groups, clips, held))
    far = other_core(mixed)
    caption_kv = caption_projection(mixed, skip, far, kv_flat, held)
    cross_out, caption_grads = cross_attention(
        core, caption_lengths, caption_order(held), mixed, caption_kv
    )
    near_terms[1], near_terms[3], caption_grads = lax.optimization_barrier(
        (near_terms[1], near_terms[3], caption_grads)
    )
    grads = tp_terms([caption_grads] * clips)
    near_terms, _ = lax.optimization_barrier((near_terms, grads[1]))
    far_terms = [other_core(x) for x in near_terms]
    kept, sent = weight_terms(near_terms, far_terms, grads, groups)

    cross_out, _, _ = lax.optimization_barrier((cross_out, self_back, sent))
    cross_back = seq_exchange(cross_out)
    self_ctx, stream_grads = unpack_self(self_back)
    taken = lax.ppermute(sent, "dp", shifts(groups, 1))
    kept, _ = lax.optimization_barrier((kept, self_ctx))
    grad = add_taken(kept, taken)
    weight_grad = grad.reshape(grad.shape[0], 2, local_width)
    cross_ctx, stream_grads = unpack_cross(cross_back, stream_grads)
    return (self_ctx, cross_ctx, stream_grads, weight_grad)


def solution(mesh):
    placed = (
        P("dp", "seq", "tp"),
        P("dp", "seq", "tp"),
        P("tp", None),
        P(),
        P(None, None, "seq"),
        P(("dp", "tp")),
        P(None, ("dp", "tp"), "seq", None),
        P(None, ("dp", "tp"), "seq", None),
    )
    return jax.shard_map(
        body,
        mesh=mesh,
        in_specs=placed,
        out_specs=(
            P(("dp", "tp"), "seq", None),
            P(("dp", "tp"), "seq", None),
            P(None, ("dp", "tp"), "seq", None),
            P(("dp", "tp"), None, "seq"),
        ),
        check_vma=False,
    )
```

```python
import functools
import math

import jax
import jax.numpy as jnp
from jax import lax
from jax.experimental import pallas as pl
from jax.experimental.pallas import tpu as pltpu
from jax.sharding import PartitionSpec as P

D_TEXT = 4096
HD = 128
SCALE = 1.0 / math.sqrt(HD)
LOG2E = math.log2(math.e)
VMEM = 56 * 2**20
SMALL = 12 * 2**20
MIDDLE = 28 * 2**20
VMEM_SELF = 36 * 2**20
ADD_COST = 2 * 10**10
CROSS_COST = 6 * 10**9
CORES = 2

NT = (((1,), (1,)), ((), ()))
NN = (((1,), (0,)), ((), ()))
TN = (((0,), (0,)), ((), ()))


def mm(a, b, dims):
    return lax.dot_general(a, b, dims, preferred_element_type=jnp.float32)


def attend_rows(queries, keys, values, cot, valid):
    scores = mm(queries, keys, NT)
    if valid is not None:
        scores = jnp.where(valid, scores, -1e30)
    top = jnp.max(scores, axis=1, keepdims=True)
    weights = jnp.exp2((scores - top) * (SCALE * LOG2E))
    inverse = 1.0 / jnp.sum(weights, axis=1, keepdims=True)
    rounded = weights.astype(jnp.bfloat16)
    context = mm(rounded, values, NN) * inverse
    products = weights * mm(cot, values, NT)
    centre = jnp.sum(products, axis=1, keepdims=True) * inverse
    grad_scores = (products - weights * centre).astype(jnp.bfloat16)
    grad_query = mm(grad_scores, keys, NN) * (inverse * SCALE)
    cot_scaled = (cot.astype(jnp.float32) * inverse).astype(jnp.bfloat16)
    query_scaled = (queries.astype(jnp.float32) * (inverse * SCALE)).astype(jnp.bfloat16)
    return (
        context,
        grad_query,
        mm(query_scaled, grad_scores, TN),
        mm(cot_scaled, rounded, TN),
    )


def self_kernel(q_ref, k_ref, v_ref, g_ref, *rest, steps, per):
    y_ref, dk_acc, dv_acc = rest[-3:]
    step = pl.program_id(0)
    blocks, _, tokens, _ = k_ref.shape
    total, rows = blocks * tokens, per * tokens

    @pl.when(step == 0)
    def _():
        dk_acc[...] = jnp.zeros_like(dk_acc)
        dv_acc[...] = jnp.zeros_like(dv_acc)

    context, grad_query, dk, dv = attend_rows(
        q_ref[...].reshape(rows, HD),
        k_ref[...].reshape(total, HD),
        v_ref[...].reshape(total, HD),
        g_ref[...].reshape(rows, HD),
        None,
    )
    at = pl.ds(step * per, per)
    y_ref[at, 0] = context.astype(jnp.bfloat16).reshape(per, tokens, HD)
    y_ref[at, 1] = grad_query.astype(jnp.bfloat16).reshape(per, tokens, HD)
    dk_acc[...] += dk
    dv_acc[...] += dv

    @pl.when(step == steps - 1)
    def _():
        y_ref[:, 2] = dk_acc[...].T.astype(jnp.bfloat16).reshape(blocks, tokens, HD)
        y_ref[:, 3] = dv_acc[...].T.astype(jnp.bfloat16).reshape(blocks, tokens, HD)


def self_attention(x, head, before):
    blocks, _, tokens, _ = x.shape
    per = max(1, 512 // tokens)
    steps = blocks // per
    total = blocks * tokens

    def rows(which):
        return pl.BlockSpec((per, 1, tokens, HD), lambda i: (i, which, 0, head))

    def whole(which):
        return pl.BlockSpec((blocks, 1, tokens, HD), lambda i: (0, which, 0, head))

    earlier = [] if before is None else [before]
    return pl.pallas_call(
        functools.partial(self_kernel, steps=steps, per=per),
        grid=(steps,),
        in_specs=[rows(0), whole(1), whole(2), rows(3)]
        + [pl.BlockSpec(memory_space=pl.ANY)] * len(earlier),
        out_specs=pl.BlockSpec((blocks, 4, tokens, HD), lambda i: (0, 0, 0, head)),
        out_shape=jax.ShapeDtypeStruct(x.shape, jnp.bfloat16),
        scratch_shapes=[pltpu.VMEM((HD, total), jnp.float32)] * 2,
        input_output_aliases={4: 0} if earlier else {},
        compiler_params=pltpu.CompilerParams(vmem_limit_bytes=VMEM_SELF),
        cost_estimate=pl.CostEstimate(
            flops=24 * total * total * HD,
            bytes_accessed=16 * total * HD,
            transcendentals=total * total,
        ),
        name="self_attention",
    )(x, x, x, x, *earlier)


def cross_kernel(core_ref, len_ref, pos_ref, x_ref, k_ref, v_ref, y_ref, d_ref, dk_acc, dv_acc):
    step = pl.program_id(0)
    total = k_ref.shape[0]

    @pl.when(step == 0)
    def _():
        dk_acc[...] = jnp.zeros_like(dk_acc)
        dv_acc[...] = jnp.zeros_like(dv_acc)

    chips, _, tokens, width = x_ref.shape
    rows = chips * CORES * tokens
    heads = width // HD
    valid = jnp.broadcast_to(pos_ref[...], (rows, total)) < len_ref[0]
    for head in range(heads):
        cols = slice(head * HD, (head + 1) * HD)
        context, grad_query, dk, dv = attend_rows(
            jnp.concatenate([x_ref[:, 0, :, cols], x_ref[:, 2, :, cols]]).reshape(rows, HD),
            k_ref[:, cols],
            v_ref[:, cols],
            jnp.concatenate([x_ref[:, 1, :, cols], x_ref[:, 3, :, cols]]).reshape(rows, HD),
            valid,
        )
        shape = (CORES, chips, tokens, HD)
        context = context.astype(jnp.bfloat16).reshape(shape)
        grad_query = grad_query.astype(jnp.bfloat16).reshape(shape)
        for chip in range(chips):
            for other in range(CORES):
                at = CORES * chip + lax.rem(core_ref[0] + other, CORES)
                y_ref[at, 0, :, cols] = context[other, chip]
                y_ref[at, 1, :, cols] = grad_query[other, chip]
        dk_acc[head] += dk
        dv_acc[head] += dv

    @pl.when(step == pl.num_programs(0) - 1)
    def _():
        for head in range(heads):
            cols = slice(head * HD, (head + 1) * HD)
            d_ref[:, cols] = dk_acc[head].T.astype(jnp.bfloat16)
            cols = slice((heads + head) * HD, (heads + head + 1) * HD)
            d_ref[:, cols] = dv_acc[head].T.astype(jnp.bfloat16)


def cross_attention(core, lengths, positions, x, kv):
    chips, _, tokens, width = x.shape
    captions = kv.shape[0]
    per = max(1, 512 // (CORES * tokens))
    heads = width // HD
    total = chips * CORES * tokens
    return pl.pallas_call(
        cross_kernel,
        grid=(chips // per,),
        in_specs=[
            pl.BlockSpec(memory_space=pltpu.SMEM),
            pl.BlockSpec(memory_space=pltpu.SMEM),
            pl.BlockSpec((1, captions), lambda i: (0, 0)),
            pl.BlockSpec((per, 2 * CORES, tokens, width), lambda i: (i, 0, 0, 0)),
            pl.BlockSpec((captions, width), lambda i: (0, 0)),
            pl.BlockSpec((captions, width), lambda i: (0, 1)),
        ],
        out_specs=[
            pl.BlockSpec((CORES * per, 2, tokens, width), lambda i: (i, 0, 0, 0)),
            pl.BlockSpec((captions, 2 * width), lambda i: (0, 0)),
        ],
        out_shape=[
            jax.ShapeDtypeStruct((CORES * chips, 2, tokens, width), jnp.bfloat16),
            jax.ShapeDtypeStruct(kv.shape, jnp.bfloat16),
        ],
        scratch_shapes=[pltpu.VMEM((heads, HD, captions), jnp.float32)] * 2,
        compiler_params=pltpu.CompilerParams(vmem_limit_bytes=MIDDLE),
        cost_estimate=pl.CostEstimate(
            flops=CROSS_COST,
            bytes_accessed=8 * total * width + 4 * kv.size,
            transcendentals=heads * total * captions,
        ),
        name="cross_attention",
    )(core, lengths, positions.reshape(1, captions), x, kv, kv)


def pack_kernel(s_ref, c_ref, x_ref, held, in_sems, out_sems):
    parts, count, _, width = x_ref.shape
    fetches, stores = [], []
    for which in range(count):
        given = s_ref.at[which, 0] if which < count - 1 else c_ref.at[0, 0]
        fetches.append(pltpu.make_async_copy(given, held.at[which], in_sems.at[which]))
        fetches[-1].start()
    for which in range(count):
        fetches[which].wait()
        for part in range(parts):
            cols = pl.ds(part * width, width)
            stores.append(
                pltpu.make_async_copy(
                    held.at[which, :, cols], x_ref.at[part, which], out_sems.at[part, which]
                )
            )
            stores[-1].start()
    for store in stores:
        store.wait()


def pack(streams, cotangents, count, parts):
    tokens, width = streams.shape[2], streams.shape[3] // parts
    return pl.pallas_call(
        pack_kernel,
        in_specs=[pl.BlockSpec(memory_space=pl.ANY)] * 2,
        out_specs=pl.BlockSpec(memory_space=pl.ANY),
        out_shape=jax.ShapeDtypeStruct((parts, count + 1, tokens, width), jnp.bfloat16),
        scratch_shapes=[
            pltpu.VMEM((count + 1, tokens, parts * width), jnp.bfloat16),
            pltpu.SemaphoreType.DMA((count + 1,)),
            pltpu.SemaphoreType.DMA((parts, count + 1)),
        ],
        compiler_params=pltpu.CompilerParams(vmem_limit_bytes=VMEM),
        cost_estimate=pl.CostEstimate(
            flops=0, bytes_accessed=4 * (count + 1) * tokens * width * parts, transcendentals=0
        ),
        name="pack",
    )(streams, cotangents)


def pack_cores_kernel(core_ref, s_ref, c_ref, keep_ref, give_ref):
    width = keep_ref.shape[3]
    for core in range(CORES):
        cols = slice(core * width, (core + 1) * width)

        @pl.when(core_ref[0] == core)
        def _():
            keep_ref[0, 0] = s_ref[0, 0, :, cols]
            keep_ref[0, 1] = c_ref[0, 0, :, cols]

        @pl.when(core_ref[0] != core)
        def _():
            give_ref[0, 0] = s_ref[0, 0, :, cols]
            give_ref[0, 1] = c_ref[0, 0, :, cols]


def pack_cores(core, streams, cotangents, stream, cot, parts):
    tokens, width = streams.shape[2], streams.shape[3] // parts
    chips = parts // CORES
    slab = pl.BlockSpec((1, 2, tokens, width), lambda j: (j, 0, 0, 0))
    return pl.pallas_call(
        pack_cores_kernel,
        grid=(chips,),
        in_specs=[
            pl.BlockSpec(memory_space=pltpu.SMEM),
            pl.BlockSpec((1, 1, tokens, CORES * width), lambda j: (stream, 0, 0, j)),
            pl.BlockSpec((1, 1, tokens, CORES * width), lambda j: (cot, 0, 0, j)),
        ],
        out_specs=[slab, slab],
        out_shape=[jax.ShapeDtypeStruct((chips, 2, tokens, width), jnp.bfloat16)] * 2,
        compiler_params=pltpu.CompilerParams(vmem_limit_bytes=VMEM),
        cost_estimate=pl.CostEstimate(
            flops=0, bytes_accessed=8 * tokens * width * parts, transcendentals=0
        ),
        name="pack_cores",
    )(core, streams, cotangents)


def unpack_self_kernel(x_ref, ctx_ref, grads_ref):
    width = x_ref.shape[3]
    for part in range(x_ref.shape[0]):
        cols = slice(part * width, (part + 1) * width)
        ctx_ref[0, :, cols] = x_ref[part, 0]
        grads_ref[:, 0, :, cols] = x_ref[part, 1:]


def unpack_self(x):
    parts, _, tokens, width = x.shape
    per = 4
    return pl.pallas_call(
        unpack_self_kernel,
        grid=(parts // per,),
        in_specs=[pl.BlockSpec((per, 4, tokens, width), lambda j: (j, 0, 0, 0))],
        out_specs=[
            pl.BlockSpec((1, tokens, per * width), lambda j: (0, 0, j)),
            pl.BlockSpec((3, 1, tokens, per * width), lambda j: (0, 0, 0, j)),
        ],
        out_shape=[
            jax.ShapeDtypeStruct((1, tokens, parts * width), jnp.bfloat16),
            jax.ShapeDtypeStruct((4, 1, tokens, parts * width), jnp.bfloat16),
        ],
        cost_estimate=pl.CostEstimate(flops=0, bytes_accessed=4 * x.size, transcendentals=0),
        compiler_params=pltpu.CompilerParams(vmem_limit_bytes=SMALL),
        name="unpack_self",
    )(x)


def unpack_cross_kernel(x_ref, _, ctx_ref, grads_ref):
    width = x_ref.shape[3]
    for part in range(x_ref.shape[0]):
        cols = slice(part * width, (part + 1) * width)
        ctx_ref[0, :, cols] = x_ref[part, 0]
        grads_ref[0, 0, :, cols] = x_ref[part, 1]


def unpack_cross(x, grads):
    parts, _, tokens, width = x.shape
    per = 4
    return pl.pallas_call(
        unpack_cross_kernel,
        grid=(parts // per,),
        in_specs=[
            pl.BlockSpec((per, 2, tokens, width), lambda j: (j, 0, 0, 0)),
            pl.BlockSpec(memory_space=pl.ANY),
        ],
        out_specs=[
            pl.BlockSpec((1, tokens, per * width), lambda j: (0, 0, j)),
            pl.BlockSpec((1, 1, tokens, per * width), lambda j: (3, 0, 0, j)),
        ],
        out_shape=[
            jax.ShapeDtypeStruct((1, tokens, parts * width), jnp.bfloat16),
            jax.ShapeDtypeStruct(grads.shape, jnp.bfloat16),
        ],
        input_output_aliases={1: 1},
        cost_estimate=pl.CostEstimate(flops=0, bytes_accessed=4 * x.size, transcendentals=0),
        compiler_params=pltpu.CompilerParams(vmem_limit_bytes=SMALL),
        name="unpack_cross",
    )(x, grads)


def project_kernel(own_ref, x_ref, w_ref, r_ref, *rest, per):
    terms, y_ref = rest[:-1], rest[-1]
    own = own_ref[0]
    y = mm(x_ref[...], w_ref[...], NN)
    mine = (pl.program_id(0) // per) == own
    y = y + jnp.where(mine, r_ref[...].astype(jnp.float32), 0.0)
    y_ref[...] = y.reshape(y_ref.shape)
    for offset, term in enumerate(terms):
        term[...] = y_ref[lax.rem(own + offset, len(terms))]


def project(context, weight, residual):
    owned, rows, depth = context.shape
    block = 512
    per = depth // block
    own = lax.axis_index("tp").astype(jnp.int32).reshape(1)
    return pl.pallas_call(
        functools.partial(project_kernel, per=per),
        grid=(weight.shape[1] // block,),
        in_specs=[
            pl.BlockSpec(memory_space=pltpu.SMEM),
            pl.BlockSpec((owned * rows, depth), lambda j: (0, 0)),
            pl.BlockSpec((depth, block), lambda j: (0, j)),
            pl.BlockSpec((owned * rows, block), lambda j: (0, lax.rem(j, per))),
        ],
        out_specs=[pl.BlockSpec((rows, block), lambda j: (0, j))] * owned,
        out_shape=[jax.ShapeDtypeStruct((rows, weight.shape[1]), jnp.float32)] * owned,
        scratch_shapes=[pltpu.VMEM((owned, rows, block), jnp.float32)],
        cost_estimate=pl.CostEstimate(
            flops=2 * owned * rows * depth * weight.shape[1],
            bytes_accessed=2 * weight.size,
            transcendentals=0,
        ),
        name="project",
    )(own, context.reshape(owned * rows, depth), weight, residual.reshape(owned * rows, depth))


def join_kernel(own_ref, other_ref, y_ref):
    y_ref[:, :2] = own_ref[...]
    y_ref[:, 2:] = other_ref[...]


def join_cores(own, other, blocks):
    chips, count, tokens, width = own.shape
    per = 2
    slab = pl.BlockSpec((per, count, tokens, width), lambda j: (j, 0, 0, 0))
    return pl.pallas_call(
        join_kernel,
        grid=(chips // per,),
        in_specs=[slab, slab],
        out_specs=pl.BlockSpec((per, 2 * count, tokens, width), lambda j: (j, 0, 0, 0)),
        out_shape=jax.ShapeDtypeStruct((chips, 2 * count + blocks, tokens, width), jnp.bfloat16),
        compiler_params=pltpu.CompilerParams(vmem_limit_bytes=SMALL),
        name="join_cores",
    )(own, other)


def norm_kernel(*refs):
    terms, (gain_ref, _, y_ref, states) = refs[:-4], refs[-4:]
    blocks, rows, width = states.shape

    @pl.when(pl.program_id(0) == 0)
    def _():
        hidden = sum(term[...] for term in terms)
        power = jnp.mean(hidden * hidden, axis=1, keepdims=True)
        normed = (hidden * lax.rsqrt(power + 1e-06) * gain_ref[...]).astype(jnp.bfloat16)
        held = terms[0].shape[0]
        per = rows // held
        for at in range(blocks * per):
            to = pl.ds(at % per * held, held)
            states[at // per, to] = normed[:, at * width : (at + 1) * width]

    for chip in range(y_ref.shape[0]):
        y_ref[chip] = states[...]


def norm_into(terms, gain, packed, blocks):
    chips, total, tokens, width = packed.shape
    rows, depth = terms[0].shape
    per = 2
    return pl.pallas_call(
        norm_kernel,
        grid=(chips // per,),
        in_specs=[pl.BlockSpec((rows, depth), lambda j: (0, 0))] * len(terms)
        + [pl.BlockSpec((1, depth), lambda j: (0, 0)), pl.BlockSpec(memory_space=pl.ANY)],
        out_specs=pl.BlockSpec(
            (per, blocks, tokens, width), lambda j: (j, total // blocks - 1, 0, 0)
        ),
        out_shape=jax.ShapeDtypeStruct(packed.shape, jnp.bfloat16),
        scratch_shapes=[pltpu.VMEM((blocks, tokens, width), jnp.bfloat16)],
        input_output_aliases={len(terms) + 1: 0},
        compiler_params=pltpu.CompilerParams(vmem_limit_bytes=SMALL),
        name="norm_into",
    )(*terms, gain.reshape(1, -1), packed)


def caption_kernel(near_ref, far_ref, w_ref, kv_ref, acc, *, held):
    step = pl.program_id(0)
    chips, _, rows, width = near_ref.shape
    half = chips * held
    for at, ref in ((0, near_ref), (half, far_ref)):
        terms = sum(
            mm(
                ref[:, 0, block * held : (block + 1) * held].reshape(half, width),
                w_ref[block * width : (block + 1) * width],
                NN,
            )
            for block in range(rows // held)
        )
        to = slice(at, at + half)

        @pl.when(step == 0)
        def _():
            acc[to] = terms

        @pl.when(step > 0)
        def _():
            acc[to] += terms

    @pl.when(step == pl.num_programs(0) - 1)
    def _():
        kv_ref[...] = acc[...].astype(jnp.bfloat16)


def caption_projection(near, skip, far, weight, held):
    chips, blocks, rows, columns = far.shape
    blocks -= skip
    captions, width = CORES * chips * held, weight.shape[1]
    depth = columns * rows // held
    return pl.pallas_call(
        functools.partial(caption_kernel, held=held),
        grid=(blocks,),
        in_specs=[
            pl.BlockSpec((chips, 1, rows, columns), lambda j: (0, skip + j, 0, 0)),
            pl.BlockSpec((chips, 1, rows, columns), lambda j: (0, skip + j, 0, 0)),
            pl.BlockSpec((depth, width), lambda j: (j, 0)),
        ],
        out_specs=pl.BlockSpec((captions, width), lambda j: (0, 0)),
        out_shape=jax.ShapeDtypeStruct((captions, width), jnp.bfloat16),
        scratch_shapes=[pltpu.VMEM((captions, width), jnp.float32)],
        compiler_params=pltpu.CompilerParams(vmem_limit_bytes=MIDDLE),
        cost_estimate=pl.CostEstimate(
            flops=2 * captions * blocks * depth * width,
            bytes_accessed=4 * far.size + 2 * weight.size,
            transcendentals=0,
        ),
        name="caption_projection",
    )(near, far, weight)


def split_kernel(own_ref, x_ref, *outs, held):
    chips, blocks, rows, columns = x_ref.shape
    per = rows // held
    count = blocks * per // len(outs)
    for clip in range(len(outs)):
        for offset, out in enumerate(outs):

            @pl.when(lax.rem(own_ref[0] + offset, len(outs)) == clip)
            def _():
                for at in range(count):
                    block, place = divmod(clip * count + at, per)
                    piece = x_ref[:, block, place * held : (place + 1) * held]
                    out[:, at * columns : (at + 1) * columns] = piece.reshape(-1, columns)


def split_features(x, skip, groups, clips, held):
    chips, blocks, rows, columns = x.shape
    blocks = (blocks - skip) // groups
    depth = blocks * columns * rows // held // clips
    own = lax.axis_index("tp").astype(jnp.int32).reshape(1)
    return pl.pallas_call(
        functools.partial(split_kernel, held=held),
        grid=(groups,),
        in_specs=[
            pl.BlockSpec(memory_space=pltpu.SMEM),
            pl.BlockSpec((chips, blocks, rows, columns), lambda d: (0, skip // blocks + d, 0, 0)),
        ],
        out_specs=[pl.BlockSpec((chips * held, depth), lambda d: (0, d))] * clips,
        out_shape=[jax.ShapeDtypeStruct((chips * held, groups * depth), x.dtype)] * clips,
        compiler_params=pltpu.CompilerParams(vmem_limit_bytes=SMALL),
        cost_estimate=pl.CostEstimate(
            flops=0, bytes_accessed=2 * x.size, transcendentals=0
        ),
        name="split_features",
    )(own, x)


def weight_kernel(own_ref, *refs, clips):
    near, far, grads = refs[:clips], refs[clips : 2 * clips], refs[2 * clips : 3 * clips]
    kept_ref, sent_ref = refs[-2:]
    half = near[0].shape[0]
    total = sum(
        mm(x[...], g[:half], TN) + mm(y[...], g[half:], TN) for x, y, g in zip(near, far, grads)
    )
    mine = pl.program_id(0) == own_ref[0]

    @pl.when(mine)
    def _():
        kept_ref[...] = total

    @pl.when(jnp.logical_not(mine))
    def _():
        sent_ref[...] = total.astype(jnp.bfloat16)


def weight_terms(near, far, grads, groups):
    clips = len(near)
    rows, width = grads[0].shape
    block = near[0].shape[1] // groups
    own = lax.axis_index("dp").astype(jnp.int32).reshape(1)
    return pl.pallas_call(
        functools.partial(weight_kernel, clips=clips),
        grid=(groups,),
        in_specs=[pl.BlockSpec(memory_space=pltpu.SMEM)]
        + [pl.BlockSpec((rows // 2, block), lambda d: (0, d))] * (2 * clips)
        + [pl.BlockSpec((rows, width), lambda d: (0, 0))] * clips,
        out_specs=[pl.BlockSpec((block, width), lambda d: (0, 0))] * 2,
        out_shape=[
            jax.ShapeDtypeStruct((block, width), jnp.float32),
            jax.ShapeDtypeStruct((block, width), jnp.bfloat16),
        ],
        compiler_params=pltpu.CompilerParams(vmem_limit_bytes=MIDDLE),
        cost_estimate=pl.CostEstimate(
            flops=2 * clips * groups * rows * block * width,
            bytes_accessed=2 * clips * rows * (groups * block + width),
            transcendentals=0,
        ),
        name="weight_terms",
    )(own, *near, *far, *grads)


def add_kernel(kept_ref, taken_ref, y_ref):
    width = y_ref.shape[2]
    for at in range(y_ref.shape[1]):
        cols = slice(at * width, (at + 1) * width)
        y_ref[:, at] = kept_ref[:, cols] + taken_ref[:, cols].astype(jnp.float32)


def add_taken(kept, taken, parts):
    rows, width = kept.shape
    steps = 4
    block = pl.BlockSpec((rows // steps, width), lambda j: (j, 0))
    return pl.pallas_call(
        add_kernel,
        grid=(steps,),
        in_specs=[block, block],
        out_specs=pl.BlockSpec((rows // steps, parts, width // parts), lambda j: (j, 0, 0)),
        out_shape=jax.ShapeDtypeStruct((rows, parts, width // parts), jnp.float32),
        compiler_params=pltpu.CompilerParams(vmem_limit_bytes=SMALL),
        cost_estimate=pl.CostEstimate(
            flops=ADD_COST, bytes_accessed=10 * kept.size, transcendentals=0
        ),
        name="add_taken",
    )(kept, taken)


def shifts(size, offset):
    return [(at, (at + offset) % size) for at in range(size)]


def seq_exchange(x):
    return lax.all_to_all(x, "seq", split_axis=0, concat_axis=0, tiled=True)


def tp_terms(terms):
    size = len(terms)
    return [terms[0]] + [
        lax.ppermute(terms[offset], "tp", shifts(size, offset)) for offset in range(1, size)
    ]


def core_exchange(x):
    size = lax.axis_size("seq")
    groups = [list(range(core, size, CORES)) for core in range(CORES)]
    return lax.all_to_all(
        x, "seq", split_axis=0, concat_axis=0, tiled=True, axis_index_groups=groups
    )


def other_core(x):
    size = lax.axis_size("seq")
    return lax.ppermute(x, "seq", [(source, source ^ 1) for source in range(size)])


def caption_order(rows):
    size, core = lax.axis_size("seq"), lax.axis_index("seq") % CORES
    chips = jnp.arange(0, size, CORES, dtype=jnp.int32)
    places = jnp.concatenate([chips + core, chips + (1 - core)])
    return (places[:, None] * rows + jnp.arange(rows, dtype=jnp.int32)[None, :]).reshape(-1)


def body(
    enc_context,
    enc_residual,
    out_weight,
    norm_gain,
    kv_weight,
    caption_lengths,
    streams,
    cotangents,
):
    parts = lax.axis_size("seq")
    groups, clips = lax.axis_size("dp"), lax.axis_size("tp")
    local_width = kv_weight.shape[2]

    held = enc_context.shape[1]
    core = (lax.axis_index("seq") % CORES).astype(jnp.int32).reshape(1)

    self_packed = pack(streams, cotangents, 3, parts)
    self_in = seq_exchange(self_packed)
    streams, cotangents, enc_context, _ = lax.optimization_barrier(
        (streams, cotangents, enc_context, self_packed)
    )
    terms = tp_terms(project(enc_context, out_weight, enc_residual))
    keep, give = pack_cores(core, streams, cotangents, 3, 1, parts)
    blocks = terms[0].size // (keep.shape[2] * keep.shape[3])
    packed = join_cores(keep, other_core(give), blocks)
    kv_flat = kv_weight.reshape(kv_weight.shape[0], 2 * local_width)
    packed, kv_flat, _ = lax.optimization_barrier(
        (norm_into(terms, norm_gain, packed, blocks), kv_flat, self_in)
    )
    mixed = core_exchange(packed)
    self_out = None
    for head in range(local_width // HD):
        self_out = self_attention(self_in, head, self_out)

    self_out, mixed = lax.optimization_barrier((self_out, mixed))
    self_back = seq_exchange(self_out)
    skip = 2 * CORES
    near_terms = tp_terms(split_features(mixed, skip, groups, clips, held))
    far = other_core(mixed)
    caption_kv = caption_projection(mixed, skip, far, kv_flat, held)
    cross_out, caption_grads = cross_attention(
        core, caption_lengths, caption_order(held), mixed, caption_kv
    )
    near_terms[1], caption_grads = lax.optimization_barrier((near_terms[1], caption_grads))
    grads = tp_terms([caption_grads] * clips)
    near_terms, _ = lax.optimization_barrier((near_terms, grads[1]))
    far_terms = [other_core(x) for x in near_terms]
    kept, sent = weight_terms(near_terms, far_terms, grads, groups)

    cross_out, _, _ = lax.optimization_barrier((cross_out, self_back, sent))
    cross_back = seq_exchange(cross_out)
    self_ctx, stream_grads = unpack_self(self_back)
    taken = lax.ppermute(sent, "dp", shifts(groups, 1))
    kept, _ = lax.optimization_barrier((kept, self_ctx))
    weight_grad = add_taken(kept, taken, 2)
    cross_ctx, stream_grads = unpack_cross(cross_back, stream_grads)
    return (self_ctx, cross_ctx, stream_grads, weight_grad)


def solution(mesh):
    placed = (
        P("dp", "seq", "tp"),
        P("dp", "seq", "tp"),
        P("tp", None),
        P(),
        P(None, None, "seq"),
        P(("dp", "tp")),
        P(None, ("dp", "tp"), "seq", None),
        P(None, ("dp", "tp"), "seq", None),
    )
    return jax.shard_map(
        body,
        mesh=mesh,
        in_specs=placed,
        out_specs=(
            P(("dp", "tp"), "seq", None),
            P(("dp", "tp"), "seq", None),
            P(None, ("dp", "tp"), "seq", None),
            P(("dp", "tp"), None, "seq"),
        ),
        check_vma=False,
    )
```

```python
import functools
import math

import jax
import jax.numpy as jnp
from jax import lax
from jax.experimental import pallas as pl
from jax.experimental.pallas import tpu as pltpu
from jax.sharding import PartitionSpec as P

D_TEXT = 4096
HD = 128
SCALE = 1.0 / math.sqrt(HD)
LOG2E = math.log2(math.e)
VMEM = 56 * 2**20
SMALL = 12 * 2**20
MIDDLE = 28 * 2**20
VMEM_SELF = 36 * 2**20
ADD_COST = 2 * 10**10
CROSS_COST = 6 * 10**9
CORES = 2
SELF_CHIPS = (0, 2, 5, 7, 1, 3, 4, 6)
CROSS_CHIPS = (0, 4, 5, 1, 2, 6, 7, 3)


def devices(chips):
    return [CORES * chip + core for chip in chips for core in range(CORES)]


NT = (((1,), (1,)), ((), ()))
NN = (((1,), (0,)), ((), ()))
TN = (((0,), (0,)), ((), ()))


def mm(a, b, dims):
    return lax.dot_general(a, b, dims, preferred_element_type=jnp.float32)


def attend_rows(queries, keys, values, cot, valid):
    scores = mm(queries, keys, NT)
    if valid is not None:
        scores = jnp.where(valid, scores, -1e30)
    top = jnp.max(scores, axis=1, keepdims=True)
    weights = jnp.exp2((scores - top) * (SCALE * LOG2E))
    inverse = 1.0 / jnp.sum(weights, axis=1, keepdims=True)
    rounded = weights.astype(jnp.bfloat16)
    context = mm(rounded, values, NN) * inverse
    products = weights * mm(cot, values, NT)
    centre = jnp.sum(products, axis=1, keepdims=True) * inverse
    grad_scores = (products - weights * centre).astype(jnp.bfloat16)
    grad_query = mm(grad_scores, keys, NN) * (inverse * SCALE)
    cot_scaled = (cot.astype(jnp.float32) * inverse).astype(jnp.bfloat16)
    query_scaled = (queries.astype(jnp.float32) * (inverse * SCALE)).astype(jnp.bfloat16)
    return (
        context,
        grad_query,
        mm(query_scaled, grad_scores, TN),
        mm(cot_scaled, rounded, TN),
    )


def self_kernel(q_ref, k_ref, v_ref, g_ref, *rest, steps, per):
    y_ref, dk_acc, dv_acc = rest[-3:]
    step = pl.program_id(0)
    blocks, _, tokens, _ = k_ref.shape
    total, rows = blocks * tokens, per * tokens

    @pl.when(step == 0)
    def _():
        dk_acc[...] = jnp.zeros_like(dk_acc)
        dv_acc[...] = jnp.zeros_like(dv_acc)

    context, grad_query, dk, dv = attend_rows(
        q_ref[...].reshape(rows, HD),
        k_ref[...].reshape(total, HD),
        v_ref[...].reshape(total, HD),
        g_ref[...].reshape(rows, HD),
        None,
    )
    at = pl.ds(step * per, per)
    y_ref[at, 0] = context.astype(jnp.bfloat16).reshape(per, tokens, HD)
    y_ref[at, 1] = grad_query.astype(jnp.bfloat16).reshape(per, tokens, HD)
    dk_acc[...] += dk
    dv_acc[...] += dv

    @pl.when(step == steps - 1)
    def _():
        y_ref[:, 2] = dk_acc[...].T.astype(jnp.bfloat16).reshape(blocks, tokens, HD)
        y_ref[:, 3] = dv_acc[...].T.astype(jnp.bfloat16).reshape(blocks, tokens, HD)


def self_attention(x, head, before):
    blocks, _, tokens, _ = x.shape
    per = max(1, 512 // tokens)
    steps = blocks // per
    total = blocks * tokens

    def rows(which):
        return pl.BlockSpec((per, 1, tokens, HD), lambda i: (i, which, 0, head))

    def whole(which):
        return pl.BlockSpec((blocks, 1, tokens, HD), lambda i: (0, which, 0, head))

    earlier = [] if before is None else [before]
    return pl.pallas_call(
        functools.partial(self_kernel, steps=steps, per=per),
        grid=(steps,),
        in_specs=[rows(0), whole(1), whole(2), rows(3)]
        + [pl.BlockSpec(memory_space=pl.ANY)] * len(earlier),
        out_specs=pl.BlockSpec((blocks, 4, tokens, HD), lambda i: (0, 0, 0, head)),
        out_shape=jax.ShapeDtypeStruct(x.shape, jnp.bfloat16),
        scratch_shapes=[pltpu.VMEM((HD, total), jnp.float32)] * 2,
        input_output_aliases={4: 0} if earlier else {},
        compiler_params=pltpu.CompilerParams(vmem_limit_bytes=VMEM_SELF),
        cost_estimate=pl.CostEstimate(
            flops=24 * total * total * HD,
            bytes_accessed=16 * total * HD,
            transcendentals=total * total,
        ),
        name="self_attention",
    )(x, x, x, x, *earlier)


def cross_kernel(core_ref, len_ref, pos_ref, x_ref, k_ref, v_ref, y_ref, d_ref, dk_acc, dv_acc):
    step = pl.program_id(0)
    total = k_ref.shape[0]

    @pl.when(step == 0)
    def _():
        dk_acc[...] = jnp.zeros_like(dk_acc)
        dv_acc[...] = jnp.zeros_like(dv_acc)

    chips, _, tokens, width = x_ref.shape
    rows = chips * CORES * tokens
    heads = width // HD
    valid = jnp.broadcast_to(pos_ref[...], (rows, total)) < len_ref[0]
    for head in range(heads):
        cols = slice(head * HD, (head + 1) * HD)
        context, grad_query, dk, dv = attend_rows(
            jnp.concatenate([x_ref[:, 0, :, cols], x_ref[:, 2, :, cols]]).reshape(rows, HD),
            k_ref[:, cols],
            v_ref[:, cols],
            jnp.concatenate([x_ref[:, 1, :, cols], x_ref[:, 3, :, cols]]).reshape(rows, HD),
            valid,
        )
        shape = (CORES, chips, tokens, HD)
        context = context.astype(jnp.bfloat16).reshape(shape)
        grad_query = grad_query.astype(jnp.bfloat16).reshape(shape)
        for chip in range(chips):
            for other in range(CORES):
                at = CORES * chip + lax.rem(core_ref[0] + other, CORES)
                y_ref[at, 0, :, cols] = context[other, chip]
                y_ref[at, 1, :, cols] = grad_query[other, chip]
        dk_acc[head] += dk
        dv_acc[head] += dv

    @pl.when(step == pl.num_programs(0) - 1)
    def _():
        for head in range(heads):
            cols = slice(head * HD, (head + 1) * HD)
            d_ref[:, cols] = dk_acc[head].T.astype(jnp.bfloat16)
            cols = slice((heads + head) * HD, (heads + head + 1) * HD)
            d_ref[:, cols] = dv_acc[head].T.astype(jnp.bfloat16)


def cross_attention(core, lengths, positions, x, kv):
    chips, _, tokens, width = x.shape
    captions = kv.shape[0]
    per = max(1, 512 // (CORES * tokens))
    heads = width // HD
    total = chips * CORES * tokens
    return pl.pallas_call(
        cross_kernel,
        grid=(chips // per,),
        in_specs=[
            pl.BlockSpec(memory_space=pltpu.SMEM),
            pl.BlockSpec(memory_space=pltpu.SMEM),
            pl.BlockSpec((1, captions), lambda i: (0, 0)),
            pl.BlockSpec((per, 2 * CORES, tokens, width), lambda i: (i, 0, 0, 0)),
            pl.BlockSpec((captions, width), lambda i: (0, 0)),
            pl.BlockSpec((captions, width), lambda i: (0, 1)),
        ],
        out_specs=[
            pl.BlockSpec((CORES * per, 2, tokens, width), lambda i: (i, 0, 0, 0)),
            pl.BlockSpec((captions, 2 * width), lambda i: (0, 0)),
        ],
        out_shape=[
            jax.ShapeDtypeStruct((CORES * chips, 2, tokens, width), jnp.bfloat16),
            jax.ShapeDtypeStruct(kv.shape, jnp.bfloat16),
        ],
        scratch_shapes=[pltpu.VMEM((heads, HD, captions), jnp.float32)] * 2,
        compiler_params=pltpu.CompilerParams(vmem_limit_bytes=MIDDLE),
        cost_estimate=pl.CostEstimate(
            flops=CROSS_COST,
            bytes_accessed=8 * total * width + 4 * kv.size,
            transcendentals=heads * total * captions,
        ),
        name="cross_attention",
    )(core, lengths, positions.reshape(1, captions), x, kv, kv)


def pack_kernel(s_ref, c_ref, x_ref, held, in_sems, out_sems, *, order):
    parts, count, _, width = x_ref.shape
    fetches, stores = [], []
    for which in range(count):
        given = s_ref.at[which, 0] if which < count - 1 else c_ref.at[0, 0]
        fetches.append(pltpu.make_async_copy(given, held.at[which], in_sems.at[which]))
        fetches[-1].start()
    for which in range(count):
        fetches[which].wait()
        for part in range(parts):
            cols = pl.ds(order[part] * width, width)
            stores.append(
                pltpu.make_async_copy(
                    held.at[which, :, cols], x_ref.at[part, which], out_sems.at[part, which]
                )
            )
            stores[-1].start()
    for store in stores:
        store.wait()


def pack(streams, cotangents, count, order):
    parts = len(order)
    tokens, width = streams.shape[2], streams.shape[3] // parts
    return pl.pallas_call(
        functools.partial(pack_kernel, order=order),
        in_specs=[pl.BlockSpec(memory_space=pl.ANY)] * 2,
        out_specs=pl.BlockSpec(memory_space=pl.ANY),
        out_shape=jax.ShapeDtypeStruct((parts, count + 1, tokens, width), jnp.bfloat16),
        scratch_shapes=[
            pltpu.VMEM((count + 1, tokens, parts * width), jnp.bfloat16),
            pltpu.SemaphoreType.DMA((count + 1,)),
            pltpu.SemaphoreType.DMA((parts, count + 1)),
        ],
        compiler_params=pltpu.CompilerParams(vmem_limit_bytes=VMEM),
        cost_estimate=pl.CostEstimate(
            flops=0, bytes_accessed=4 * (count + 1) * tokens * width * parts, transcendentals=0
        ),
        name="pack",
    )(streams, cotangents)


def pack_cores_kernel(core_ref, s_ref, c_ref, keep_ref, give_ref, *, order):
    width = keep_ref.shape[3]
    for at, chip in enumerate(order):
        for core in range(CORES):
            place = CORES * chip + core
            cols = slice(place * width, (place + 1) * width)

            @pl.when(core_ref[0] == core)
            def _():
                keep_ref[at, 0] = s_ref[0, 0, :, cols]
                keep_ref[at, 1] = c_ref[0, 0, :, cols]

            @pl.when(core_ref[0] != core)
            def _():
                give_ref[at, 0] = s_ref[0, 0, :, cols]
                give_ref[at, 1] = c_ref[0, 0, :, cols]


def pack_cores(core, streams, cotangents, stream, cot, order):
    chips = len(order)
    tokens, columns = streams.shape[2:]
    width = columns // (CORES * chips)
    rows = 32
    slab = pl.BlockSpec((chips, 2, rows, width), lambda j: (0, 0, j, 0))
    return pl.pallas_call(
        functools.partial(pack_cores_kernel, order=order),
        grid=(tokens // rows,),
        in_specs=[
            pl.BlockSpec(memory_space=pltpu.SMEM),
            pl.BlockSpec((1, 1, rows, columns), lambda j: (stream, 0, j, 0)),
            pl.BlockSpec((1, 1, rows, columns), lambda j: (cot, 0, j, 0)),
        ],
        out_specs=[slab, slab],
        out_shape=[jax.ShapeDtypeStruct((chips, 2, tokens, width), jnp.bfloat16)] * 2,
        compiler_params=pltpu.CompilerParams(vmem_limit_bytes=VMEM),
        cost_estimate=pl.CostEstimate(
            flops=0, bytes_accessed=8 * tokens * columns, transcendentals=0
        ),
        name="pack_cores",
    )(core, streams, cotangents)


def unpack_self_kernel(x_ref, ctx_ref, grads_ref, *, order):
    width = x_ref.shape[3]
    for at, place in enumerate(order):
        cols = slice(place * width, (place + 1) * width)
        ctx_ref[0, :, cols] = x_ref[at, 0]
        grads_ref[:, 0, :, cols] = x_ref[at, 1:]


def unpack_self(x, order):
    parts, _, tokens, width = x.shape
    rows = 32
    return pl.pallas_call(
        functools.partial(unpack_self_kernel, order=order),
        grid=(tokens // rows,),
        in_specs=[pl.BlockSpec((parts, 4, rows, width), lambda j: (0, 0, j, 0))],
        out_specs=[
            pl.BlockSpec((1, rows, parts * width), lambda j: (0, j, 0)),
            pl.BlockSpec((3, 1, rows, parts * width), lambda j: (0, 0, j, 0)),
        ],
        out_shape=[
            jax.ShapeDtypeStruct((1, tokens, parts * width), jnp.bfloat16),
            jax.ShapeDtypeStruct((4, 1, tokens, parts * width), jnp.bfloat16),
        ],
        compiler_params=pltpu.CompilerParams(vmem_limit_bytes=SMALL),
        cost_estimate=pl.CostEstimate(flops=0, bytes_accessed=4 * x.size, transcendentals=0),
        name="unpack_self",
    )(x)


def unpack_cross_kernel(x_ref, _, ctx_ref, grads_ref, *, order):
    width = x_ref.shape[3]
    for at, place in enumerate(order):
        cols = slice(place * width, (place + 1) * width)
        ctx_ref[0, :, cols] = x_ref[at, 0]
        grads_ref[0, 0, :, cols] = x_ref[at, 1]


def unpack_cross(x, grads, order):
    parts, _, tokens, width = x.shape
    rows = 32
    return pl.pallas_call(
        functools.partial(unpack_cross_kernel, order=order),
        grid=(tokens // rows,),
        in_specs=[
            pl.BlockSpec((parts, 2, rows, width), lambda j: (0, 0, j, 0)),
            pl.BlockSpec(memory_space=pl.ANY),
        ],
        out_specs=[
            pl.BlockSpec((1, rows, parts * width), lambda j: (0, j, 0)),
            pl.BlockSpec((1, 1, rows, parts * width), lambda j: (3, 0, j, 0)),
        ],
        out_shape=[
            jax.ShapeDtypeStruct((1, tokens, parts * width), jnp.bfloat16),
            jax.ShapeDtypeStruct(grads.shape, jnp.bfloat16),
        ],
        input_output_aliases={1: 1},
        compiler_params=pltpu.CompilerParams(vmem_limit_bytes=SMALL),
        cost_estimate=pl.CostEstimate(flops=0, bytes_accessed=4 * x.size, transcendentals=0),
        name="unpack_cross",
    )(x, grads)


def project_kernel(own_ref, x_ref, w_ref, r_ref, *rest, per):
    terms, y_ref = rest[:-1], rest[-1]
    own = own_ref[0]
    y = mm(x_ref[...], w_ref[...], NN)
    mine = (pl.program_id(0) // per) == own
    y = y + jnp.where(mine, r_ref[...].astype(jnp.float32), 0.0)
    y_ref[...] = y.reshape(y_ref.shape)
    for offset, term in enumerate(terms):
        term[...] = y_ref[lax.rem(own + offset, len(terms))]


def project(context, weight, residual):
    owned, rows, depth = context.shape
    block = 512
    per = depth // block
    own = lax.axis_index("tp").astype(jnp.int32).reshape(1)
    return pl.pallas_call(
        functools.partial(project_kernel, per=per),
        grid=(weight.shape[1] // block,),
        in_specs=[
            pl.BlockSpec(memory_space=pltpu.SMEM),
            pl.BlockSpec((owned * rows, depth), lambda j: (0, 0)),
            pl.BlockSpec((depth, block), lambda j: (0, j)),
            pl.BlockSpec((owned * rows, block), lambda j: (0, lax.rem(j, per))),
        ],
        out_specs=[pl.BlockSpec((rows, block), lambda j: (0, j))] * owned,
        out_shape=[jax.ShapeDtypeStruct((rows, weight.shape[1]), jnp.float32)] * owned,
        scratch_shapes=[pltpu.VMEM((owned, rows, block), jnp.float32)],
        cost_estimate=pl.CostEstimate(
            flops=2 * owned * rows * depth * weight.shape[1],
            bytes_accessed=2 * weight.size,
            transcendentals=0,
        ),
        name="project",
    )(own, context.reshape(owned * rows, depth), weight, residual.reshape(owned * rows, depth))


def join_kernel(own_ref, other_ref, y_ref):
    y_ref[:, :2] = own_ref[...]
    y_ref[:, 2:] = other_ref[...]


def join_cores(own, other, blocks):
    chips, count, tokens, width = own.shape
    per = 2
    slab = pl.BlockSpec((per, count, tokens, width), lambda j: (j, 0, 0, 0))
    return pl.pallas_call(
        join_kernel,
        grid=(chips // per,),
        in_specs=[slab, slab],
        out_specs=pl.BlockSpec((per, 2 * count, tokens, width), lambda j: (j, 0, 0, 0)),
        out_shape=jax.ShapeDtypeStruct((chips, 2 * count + blocks, tokens, width), jnp.bfloat16),
        compiler_params=pltpu.CompilerParams(vmem_limit_bytes=SMALL),
        name="join_cores",
    )(own, other)


def norm_kernel(*refs):
    terms, (gain_ref, _, y_ref, states) = refs[:-4], refs[-4:]
    blocks, rows, width = states.shape

    @pl.when(pl.program_id(0) == 0)
    def _():
        hidden = sum(term[...] for term in terms)
        power = jnp.mean(hidden * hidden, axis=1, keepdims=True)
        normed = (hidden * lax.rsqrt(power + 1e-06) * gain_ref[...]).astype(jnp.bfloat16)
        held = terms[0].shape[0]
        per = rows // held
        for at in range(blocks * per):
            to = pl.ds(at % per * held, held)
            states[at // per, to] = normed[:, at * width : (at + 1) * width]

    for chip in range(y_ref.shape[0]):
        y_ref[chip] = states[...]


def norm_into(terms, gain, packed, blocks):
    chips, total, tokens, width = packed.shape
    rows, depth = terms[0].shape
    per = 2
    return pl.pallas_call(
        norm_kernel,
        grid=(chips // per,),
        in_specs=[pl.BlockSpec((rows, depth), lambda j: (0, 0))] * len(terms)
        + [pl.BlockSpec((1, depth), lambda j: (0, 0)), pl.BlockSpec(memory_space=pl.ANY)],
        out_specs=pl.BlockSpec(
            (per, blocks, tokens, width), lambda j: (j, total // blocks - 1, 0, 0)
        ),
        out_shape=jax.ShapeDtypeStruct(packed.shape, jnp.bfloat16),
        scratch_shapes=[pltpu.VMEM((blocks, tokens, width), jnp.bfloat16)],
        input_output_aliases={len(terms) + 1: 0},
        compiler_params=pltpu.CompilerParams(vmem_limit_bytes=SMALL),
        name="norm_into",
    )(*terms, gain.reshape(1, -1), packed)


def caption_kernel(near_ref, far_ref, w_ref, kv_ref, acc, *, held):
    step = pl.program_id(0)
    chips, _, rows, width = near_ref.shape
    half = chips * held
    for at, ref in ((0, near_ref), (half, far_ref)):
        terms = sum(
            mm(
                ref[:, 0, block * held : (block + 1) * held].reshape(half, width),
                w_ref[block * width : (block + 1) * width],
                NN,
            )
            for block in range(rows // held)
        )
        to = slice(at, at + half)

        @pl.when(step == 0)
        def _():
            acc[to] = terms

        @pl.when(step > 0)
        def _():
            acc[to] += terms

    @pl.when(step == pl.num_programs(0) - 1)
    def _():
        kv_ref[...] = acc[...].astype(jnp.bfloat16)


def caption_projection(near, skip, far, weight, held):
    chips, blocks, rows, columns = far.shape
    blocks -= skip
    captions, width = CORES * chips * held, weight.shape[1]
    depth = columns * rows // held
    return pl.pallas_call(
        functools.partial(caption_kernel, held=held),
        grid=(blocks,),
        in_specs=[
            pl.BlockSpec((chips, 1, rows, columns), lambda j: (0, skip + j, 0, 0)),
            pl.BlockSpec((chips, 1, rows, columns), lambda j: (0, skip + j, 0, 0)),
            pl.BlockSpec((depth, width), lambda j: (j, 0)),
        ],
        out_specs=pl.BlockSpec((captions, width), lambda j: (0, 0)),
        out_shape=jax.ShapeDtypeStruct((captions, width), jnp.bfloat16),
        scratch_shapes=[pltpu.VMEM((captions, width), jnp.float32)],
        compiler_params=pltpu.CompilerParams(vmem_limit_bytes=MIDDLE),
        cost_estimate=pl.CostEstimate(
            flops=2 * captions * blocks * depth * width,
            bytes_accessed=4 * far.size + 2 * weight.size,
            transcendentals=0,
        ),
        name="caption_projection",
    )(near, far, weight)


def split_kernel(own_ref, x_ref, *outs, held):
    chips, blocks, rows, columns = x_ref.shape
    per = rows // held
    count = blocks * per // len(outs)
    for clip in range(len(outs)):
        for offset, out in enumerate(outs):

            @pl.when(lax.rem(own_ref[0] + offset, len(outs)) == clip)
            def _():
                for at in range(count):
                    block, place = divmod(clip * count + at, per)
                    piece = x_ref[:, block, place * held : (place + 1) * held]
                    out[:, at * columns : (at + 1) * columns] = piece.reshape(-1, columns)


def split_features(x, skip, groups, clips, held):
    chips, blocks, rows, columns = x.shape
    blocks = (blocks - skip) // groups
    depth = blocks * columns * rows // held // clips
    own = lax.axis_index("tp").astype(jnp.int32).reshape(1)
    return pl.pallas_call(
        functools.partial(split_kernel, held=held),
        grid=(groups,),
        in_specs=[
            pl.BlockSpec(memory_space=pltpu.SMEM),
            pl.BlockSpec((chips, blocks, rows, columns), lambda d: (0, skip // blocks + d, 0, 0)),
        ],
        out_specs=[pl.BlockSpec((chips * held, depth), lambda d: (0, d))] * clips,
        out_shape=[jax.ShapeDtypeStruct((chips * held, groups * depth), x.dtype)] * clips,
        compiler_params=pltpu.CompilerParams(vmem_limit_bytes=SMALL),
        cost_estimate=pl.CostEstimate(
            flops=0, bytes_accessed=2 * x.size, transcendentals=0
        ),
        name="split_features",
    )(own, x)


def weight_kernel(own_ref, *refs, clips):
    near, far, grads = refs[:clips], refs[clips : 2 * clips], refs[2 * clips : 3 * clips]
    kept_ref, sent_ref = refs[-2:]
    half = near[0].shape[0]
    total = sum(
        mm(x[...], g[:half], TN) + mm(y[...], g[half:], TN) for x, y, g in zip(near, far, grads)
    )
    mine = pl.program_id(0) == own_ref[0]

    @pl.when(mine)
    def _():
        kept_ref[...] = total

    @pl.when(jnp.logical_not(mine))
    def _():
        sent_ref[...] = total.astype(jnp.bfloat16)


def weight_terms(near, far, grads, groups):
    clips = len(near)
    rows, width = grads[0].shape
    block = near[0].shape[1] // groups
    own = lax.axis_index("dp").astype(jnp.int32).reshape(1)
    return pl.pallas_call(
        functools.partial(weight_kernel, clips=clips),
        grid=(groups,),
        in_specs=[pl.BlockSpec(memory_space=pltpu.SMEM)]
        + [pl.BlockSpec((rows // 2, block), lambda d: (0, d))] * (2 * clips)
        + [pl.BlockSpec((rows, width), lambda d: (0, 0))] * clips,
        out_specs=[pl.BlockSpec((block, width), lambda d: (0, 0))] * 2,
        out_shape=[
            jax.ShapeDtypeStruct((block, width), jnp.float32),
            jax.ShapeDtypeStruct((block, width), jnp.bfloat16),
        ],
        compiler_params=pltpu.CompilerParams(vmem_limit_bytes=MIDDLE),
        cost_estimate=pl.CostEstimate(
            flops=2 * clips * groups * rows * block * width,
            bytes_accessed=2 * clips * rows * (groups * block + width),
            transcendentals=0,
        ),
        name="weight_terms",
    )(own, *near, *far, *grads)


def add_kernel(kept_ref, taken_ref, y_ref):
    width = y_ref.shape[2]
    for at in range(y_ref.shape[1]):
        cols = slice(at * width, (at + 1) * width)
        y_ref[:, at] = kept_ref[:, cols] + taken_ref[:, cols].astype(jnp.float32)


def add_taken(kept, taken, parts):
    rows, width = kept.shape
    steps = 4
    block = pl.BlockSpec((rows // steps, width), lambda j: (j, 0))
    return pl.pallas_call(
        add_kernel,
        grid=(steps,),
        in_specs=[block, block],
        out_specs=pl.BlockSpec((rows // steps, parts, width // parts), lambda j: (j, 0, 0)),
        out_shape=jax.ShapeDtypeStruct((rows, parts, width // parts), jnp.float32),
        compiler_params=pltpu.CompilerParams(vmem_limit_bytes=SMALL),
        cost_estimate=pl.CostEstimate(
            flops=ADD_COST, bytes_accessed=10 * kept.size, transcendentals=0
        ),
        name="add_taken",
    )(kept, taken)


def shifts(size, offset):
    return [(at, (at + offset) % size) for at in range(size)]


def seq_exchange(x, order):
    return lax.all_to_all(
        x, "seq", split_axis=0, concat_axis=0, tiled=True, axis_index_groups=[order]
    )


def tp_terms(terms):
    size = len(terms)
    return [terms[0]] + [
        lax.ppermute(terms[offset], "tp", shifts(size, offset)) for offset in range(1, size)
    ]


def core_exchange(x):
    groups = [[CORES * chip + core for chip in CROSS_CHIPS] for core in range(CORES)]
    return lax.all_to_all(
        x, "seq", split_axis=0, concat_axis=0, tiled=True, axis_index_groups=groups
    )


def other_core(x):
    size = lax.axis_size("seq")
    return lax.ppermute(x, "seq", [(source, source ^ 1) for source in range(size)])


def caption_order(rows):
    core = lax.axis_index("seq") % CORES
    chips = CORES * jnp.asarray(CROSS_CHIPS, jnp.int32)
    places = jnp.concatenate([chips + core, chips + (1 - core)])
    return (places[:, None] * rows + jnp.arange(rows, dtype=jnp.int32)[None, :]).reshape(-1)


def body(
    enc_context,
    enc_residual,
    out_weight,
    norm_gain,
    kv_weight,
    caption_lengths,
    streams,
    cotangents,
):
    groups, clips = lax.axis_size("dp"), lax.axis_size("tp")
    local_width = kv_weight.shape[2]

    held = enc_context.shape[1]
    core = (lax.axis_index("seq") % CORES).astype(jnp.int32).reshape(1)

    self_packed = pack(streams, cotangents, 3, devices(SELF_CHIPS))
    self_in = seq_exchange(self_packed, devices(SELF_CHIPS))
    streams, cotangents, enc_context, _ = lax.optimization_barrier(
        (streams, cotangents, enc_context, self_packed)
    )
    terms = tp_terms(project(enc_context, out_weight, enc_residual))
    keep, give = pack_cores(core, streams, cotangents, 3, 1, CROSS_CHIPS)
    blocks = terms[0].size // (keep.shape[2] * keep.shape[3])
    packed = join_cores(keep, other_core(give), blocks)
    kv_flat = kv_weight.reshape(kv_weight.shape[0], 2 * local_width)
    packed, kv_flat, _ = lax.optimization_barrier(
        (norm_into(terms, norm_gain, packed, blocks), kv_flat, self_in)
    )
    mixed = core_exchange(packed)
    self_out = None
    for head in range(local_width // HD):
        self_out = self_attention(self_in, head, self_out)

    self_out, mixed = lax.optimization_barrier((self_out, mixed))
    self_back = seq_exchange(self_out, devices(SELF_CHIPS))
    skip = 2 * CORES
    near_terms = tp_terms(split_features(mixed, skip, groups, clips, held))
    far = other_core(mixed)
    caption_kv = caption_projection(mixed, skip, far, kv_flat, held)
    cross_out, caption_grads = cross_attention(
        core, caption_lengths, caption_order(held), mixed, caption_kv
    )
    near_terms[1], caption_grads = lax.optimization_barrier((near_terms[1], caption_grads))
    grads = tp_terms([caption_grads] * clips)
    near_terms, _ = lax.optimization_barrier((near_terms, grads[1]))
    far_terms = [other_core(x) for x in near_terms]
    kept, sent = weight_terms(near_terms, far_terms, grads, groups)

    cross_out, _, _ = lax.optimization_barrier((cross_out, self_back, sent))
    cross_back = seq_exchange(cross_out, devices(CROSS_CHIPS))
    self_ctx, stream_grads = unpack_self(self_back, devices(SELF_CHIPS))
    taken = lax.ppermute(sent, "dp", shifts(groups, 1))
    kept, _ = lax.optimization_barrier((kept, self_ctx))
    weight_grad = add_taken(kept, taken, 2)
    cross_ctx, stream_grads = unpack_cross(cross_back, stream_grads, devices(CROSS_CHIPS))
    return (self_ctx, cross_ctx, stream_grads, weight_grad)


def solution(mesh):
    placed = (
        P("dp", "seq", "tp"),
        P("dp", "seq", "tp"),
        P("tp", None),
        P(),
        P(None, None, "seq"),
        P(("dp", "tp")),
        P(None, ("dp", "tp"), "seq", None),
        P(None, ("dp", "tp"), "seq", None),
    )
    return jax.shard_map(
        body,
        mesh=mesh,
        in_specs=placed,
        out_specs=(
            P(("dp", "tp"), "seq", None),
            P(("dp", "tp"), "seq", None),
            P(None, ("dp", "tp"), "seq", None),
            P(("dp", "tp"), None, "seq"),
        ),
        check_vma=False,
    )
```
